512 devices in a mesh: head: 32 (over x, z_lo), blk: 16 (over z_hi, y, core).
Axes of the slice: x: 4, y: 4, z: 16 (z_hi: 2, z_lo: 8; z = z_hi * 8 + z_lo), core: 2. Of those that a mesh axis runs over, the one named last changes fastest.
Arguments:
- queries: bfloat16 [12288, 4096], P('blk', 'head'), may hold values from -6 to 6
- key_states: bfloat16 [12288, 4096], P('blk', 'head'), may hold values from -6 to 6
- value_states: bfloat16 [12288, 4096], P('blk', 'head'), may hold values from -6 to 6
Outputs:
- attended: bfloat16 [12288, 4096], P(('blk', 'head'))
- heavy_scores: float32 [32, 12288], P('head', 'blk')
The draws below stay inside these ranges and needn't reach their ends.
All inputs are finite; a program needn't handle non-finite values.
Results may differ from the reference program's by a relative error of at most 0.0085.
Values may be sent and summed in bfloat16 or wider, within the bound.
A program may use at most 64 MiB of HBM per device.

```python
import math
import jax
import jax.numpy as jnp
from jax import lax

HEAD_DIM = 128
HEADS = 32
D = 4096
BLK = 768
SEQ = 12288
N_BLK = 16


def draw_queries(key, part):
    key = jax.random.fold_in(key, 3)
    values = jnp.clip(jax.random.normal(key, (SEQ, D), jnp.float32), -6.0, 6.0)
    return values.astype(jnp.bfloat16)


def draw_key_states(key, part):
    key = jax.random.fold_in(key, 5)
    values = jnp.clip(jax.random.normal(key, (SEQ, D), jnp.float32), -6.0, 6.0)
    return values.astype(jnp.bfloat16)


def block_scale(own_key, shape, pieces, low, high):
    level, own = 1.0, jax.random.fold_in(own_key, 6)
    for position, parts in pieces:
        draws = jnp.exp(jax.random.uniform(jax.random.fold_in(own, position), (parts,), jnp.float32, low / len(pieces), high / len(pieces)))
        level = level * jnp.repeat(draws, shape[position] // parts).reshape([-1 if axis == position else 1 for axis in range(len(shape))])
    return level


def scatter_about(key, dims, scale, bound, split=(), kind=jnp.bfloat16):
    level = block_scale(key, dims, split, -0.22, 0.18) if split else 1.0
    values = jax.random.normal(key, dims, jnp.float32) * scale * level
    return jnp.minimum(jnp.maximum(values, -bound), bound).astype(kind)


def setup_inputs(seed: int = 0) -> dict:
    arg_keys = jax.random.split(jax.random.key(seed), 4)
    queries = draw_queries(jax.random.fold_in(arg_keys[3], 71), 0)
    key_states = draw_key_states(jax.random.fold_in(arg_keys[3], 71), 0)
    value_states = scatter_about(arg_keys[2], (SEQ, D), 1.0, 6.0, ((0, 16), (1, 32)))
    return dict(queries=queries, key_states=key_states, value_states=value_states)


def reference(queries, key_states, value_states):
    scaling = 1.0 / math.sqrt(HEAD_DIM)

    def split_heads(matrix):
        return matrix.reshape(SEQ, HEADS, HEAD_DIM).transpose(1, 0, 2).astype(jnp.float32)
    query_all = split_heads(queries)
    key_all = split_heads(key_states)
    value_all = split_heads(value_states)
    key_pos = jnp.arange(SEQ, dtype=jnp.int32)

    def head_work(operands):
        query_head, key_head, value_head = operands

        def block_step(column_acc, block_idx):
            begin_row = (block_idx * BLK).astype(jnp.int32)
            query_block = lax.dynamic_slice_in_dim(query_head, begin_row, BLK, 0)
            logits = jnp.dot(query_block, key_head.T, precision=lax.Precision.HIGHEST) * scaling
            query_pos = begin_row + jnp.arange(BLK, dtype=jnp.int32)
            visible = key_pos[None, :] <= query_pos[:, None]
            logits = jnp.where(visible, logits, -jnp.inf)
            rowmax = lax.optimization_barrier(jnp.max(logits, axis=1, keepdims=True))
            expo = jnp.where(visible, jnp.exp(logits - rowmax), jnp.float32(0.0))
            total = lax.optimization_barrier(jnp.sum(expo, axis=1, keepdims=True))
            weights = lax.optimization_barrier(expo.astype(jnp.bfloat16)).astype(jnp.float32)
            output = jnp.dot(weights, value_head, precision=lax.Precision.HIGHEST) / total
            column_acc = column_acc + lax.optimization_barrier(jnp.sum(expo / total, axis=0))
            return (column_acc, output.astype(jnp.bfloat16))
        column_acc, outputs = lax.scan(block_step, jnp.zeros((SEQ,), jnp.float32), jnp.arange(N_BLK, dtype=jnp.int32))
        return (column_acc, outputs.reshape(SEQ, HEAD_DIM))
    heavy_scores, outputs = lax.map(head_work, (query_all, key_all, value_all))
    attended = outputs.transpose(1, 0, 2).reshape(SEQ, D)
    return (attended, heavy_scores)
```

```python
import functools
import math

import jax
import jax.numpy as jnp
from jax import lax
from jax.experimental import pallas as pl
from jax.experimental.pallas import tpu as pltpu
from jax.sharding import PartitionSpec as P

MESH = pl.DeviceIdType.MESH
DIM = 128
ROWS = 768
HEADS = 32
HALF = 8
CHUNK = 192
CHUNKS = ROWS // CHUNK
GROUP = ROWS // HEADS
GROUPS = CHUNK // GROUP
TILE = 384
WIDE = 1536
SCALE = math.log2(math.e) / math.sqrt(DIM)
LOW = -1e30


def dot_rows(a, b):
    return lax.dot_general(a, b, (((1,), (1,)), ((), ())), preferred_element_type=jnp.float32)


def dot(a, b):
    return lax.dot_general(a, b, (((1,), (0,)), ((), ())), preferred_element_type=jnp.float32)


def fold_lanes(value, op):
    out = value[:, :128]
    for u in range(1, value.shape[1] // 128):
        out = op(out, value[:, u * 128 : (u + 1) * 128])
    return out


def weigh(logits, values):
    top = jnp.max(fold_lanes(logits, jnp.maximum), axis=1, keepdims=True)
    expo = jnp.exp2((logits - top) * SCALE)
    total = fold_lanes(expo, jnp.add)
    weights = expo.astype(jnp.bfloat16)
    return top, total, weights, dot(weights, values)


def to_lanes(column):
    out = []
    for begin, size in ((0, 128), (128, 64)):
        part = column[begin : begin + size]
        row = lax.broadcasted_iota(jnp.int32, part.shape, 0)
        lane = lax.broadcasted_iota(jnp.int32, part.shape, 1)
        out.append(jnp.sum(jnp.where(row == lane, part, 0.0), axis=0, keepdims=True))
    return out


def to_column(row):
    parts = []
    for begin, size in ((0, 128), (128, 64)):
        square = jnp.broadcast_to(row[:, begin : begin + 128], (128, 128))
        parts.append(jnp.transpose(square)[:size])
    return jnp.concatenate(parts, axis=0)


def kernel(
    q_ref, k_ref, v_ref, att_ref, heavy_ref,
    keys, values, q_far, weights_tri, top_tri, total_tri, out_tri,
    weights_far, top_far, total_far, out_far, lse_col,
    send_own, send_far, stat_own, stat_far, stat_peer,
    got_own, got_far, got_stat_own, got_stat_far, turned_a, turned_b,
    column, column_out, column_in,
    k_send, k_recv, v_send, v_recv, q_send, q_recv,
    own_send, own_recv, own_stat_send, own_stat_recv,
    far_send, far_recv, far_stat_send, far_stat_recv,
    peer_send, peer_recv, col_send, col_recv,
):
    h = lax.axis_index("head")
    b = lax.axis_index("blk")
    later = b // HALF
    w = lax.rem(b, HALF)
    y, core = w // 2, lax.rem(w, 2)
    x, z = h // 8, lax.rem(h, 8)
    base = later * HALF
    is_early, is_late = later == 0, later == 1

    def place(dy, flip):
        yy = lax.rem(y + dy, 4)
        return yy * 2 + (lax.rem(core + flip, 2))

    def half_device(block):
        return (h, base + block)

    partner = (h, w + (1 - later) * HALF)
    w_right, w_left, w_core = place(1, 0), place(3, 0), place(0, 1)

    def copy(src, dst, send_sem, recv_sem, device):
        return pltpu.make_async_remote_copy(
            src_ref=src, dst_ref=dst, send_sem=send_sem, recv_sem=recv_sem,
            device_id=device, device_id_type=MESH,
        )

    barrier = pltpu.get_barrier_semaphore()

    def greet(device):
        pl.semaphore_signal(barrier, inc=1, device_id=device, device_id_type=MESH)

    def greet_far(j, carry):
        greet((lax.rem(h + j, HEADS), w + (1 - later) * HALF))
        return carry

    def greet_heads(j, carry):
        greet((lax.rem(h + j, HEADS), b))
        return carry

    def greet_half(j, carry):
        greet((h, base + lax.rem(w + j, HALF)))
        return carry

    lax.fori_loop(0, HEADS, greet_far, 0)
    lax.fori_loop(1, HEADS, greet_heads, 0)
    lax.fori_loop(1, HALF, greet_half, 0)

    keys[w] = k_ref[...]
    values[w] = v_ref[...]

    def triangle(block, masked):
        for t in range(ROWS // TILE):
            rows = pl.ds(t * TILE, TILE)
            logits = dot_rows(q_ref[rows, :], keys[block])
            if masked:
                row = lax.broadcasted_iota(jnp.int32, logits.shape, 0) + t * TILE
                col = lax.broadcasted_iota(jnp.int32, logits.shape, 1)
                logits = jnp.where(col <= row, logits, LOW)
            top, total, weights, out = weigh(logits, values[block])
            weights_tri[block, rows, :] = weights
            top_tri[block, rows, :] = jnp.broadcast_to(top, (TILE, 128))
            total_tri[block, rows, :] = total
            out_tri[block, rows, :] = out

    triangle(w, True)
    column[...] = jnp.zeros_like(column)

    pl.semaphore_wait(barrier, 2 * HEADS - 1 + HALF - 1)

    def q_copy(ci):
        rows = pl.ds(pl.multiple_of(ci * CHUNK, CHUNK), CHUNK)
        return copy(q_ref.at[rows], q_far.at[rows], q_send.at[ci], q_recv.at[ci], partner)

    @pl.when(is_late)
    def _():
        def start(i, carry):
            q_copy(lax.rem(x + i, CHUNKS)).start()
            return carry

        lax.fori_loop(0, CHUNKS, start, 0)

    def k_copy(block, slot, to):
        return copy(keys.at[block], keys.at[block], k_send.at[slot], k_recv.at[block], half_device(to))

    def v_copy(block, slot, to):
        return copy(values.at[block], values.at[block], v_send.at[slot], v_recv.at[block], half_device(to))

    k_copy(w, 0, w_right).start()
    k_copy(w, 1, w_left).start()
    k_copy(w, 2, w_core).start()
    v_copy(w, 0, w_right).start()
    v_copy(w, 1, w_left).start()
    v_copy(w, 2, w_core).start()

    def k_wait(block):
        k_copy(block, 0, w_core).wait_recv()

    def v_wait(block):
        v_copy(block, 0, w_core).wait_recv()

    def own_copy(hg):
        return copy(send_own.at[hg], got_own.at[h], own_send.at[hg], own_recv.at[h], (hg, b))

    def own_stat_copy(hg):
        return copy(
            stat_own.at[hg // GROUPS], got_stat_own.at[h],
            own_stat_send.at[hg], own_stat_recv.at[h], (hg, b),
        )

    def far_copy(hg):
        return copy(send_far.at[hg], got_far.at[h], far_send.at[hg], far_recv.at[h], (hg, w + HALF))

    def far_stat_copy(hg):
        return copy(
            stat_far.at[hg // GROUPS], got_stat_far.at[h],
            far_stat_send.at[hg], far_stat_recv.at[h], (hg, w + HALF),
        )

    def peer_copy(stat, ci):
        return copy(stat.at[ci], stat_peer.at[ci], peer_send.at[ci], peer_recv.at[ci], partner)

    def settle(count, rows, tops, totals, outs):
        top = lax.fori_loop(
            1, count, lambda j, top: jnp.maximum(top, tops[j, rows, :]), tops[0, rows, :]
        )

        def add(j, carry):
            total, out = carry
            factor = jnp.exp2((tops[j, rows, :] - top) * SCALE)
            return (total + factor * totals[j, rows, :], out + factor * outs[j, rows, :])

        zero = jnp.zeros((CHUNK, 128), jnp.float32)
        total, out = lax.fori_loop(0, count, add, (zero, zero))
        total = jnp.sum(total, axis=1, keepdims=True)
        return out * (1.0 / total), top * SCALE + jnp.log2(total)

    def settle_triangle():
        def chunk(ci, carry):
            rows = pl.ds(pl.multiple_of(ci * CHUNK, CHUNK), CHUNK)
            out, lse = settle(w + 1, rows, top_tri, total_tri, out_tri)
            send_own[pl.ds(ci * GROUPS, GROUPS)] = out.reshape(GROUPS, GROUP, DIM).astype(jnp.bfloat16)
            lse_col[rows, :] = lse
            low, high = to_lanes(lse)
            stat_own[ci, :, :128] = low
            stat_own[ci, :, 128:] = high
            return carry

        lax.fori_loop(0, CHUNKS, chunk, 0)

        @pl.when(is_late)
        def _():
            for ci in range(CHUNKS):
                peer_copy(stat_own, ci).start()

        got_own[h] = send_own[h]

        def start(j, carry):
            hg = lax.rem(h + j, HEADS)
            own_copy(hg).start()

            @pl.when(is_late)
            def _():
                own_stat_copy(hg).start()

            return carry

        lax.fori_loop(1, HEADS, start, 0)

        @pl.when(is_late)
        def _():
            got_stat_own[h] = stat_own[h // GROUPS]

    def rectangle(ci):
        q_copy(ci).wait_recv()
        rows = pl.ds(pl.multiple_of(ci * CHUNK, CHUNK), CHUNK)
        local = pl.ds(0, CHUNK)

        def step(d, carry):
            key_tile = keys[pl.ds(d * 2, 2)].reshape(WIDE, DIM)
            value_tile = values[pl.ds(d * 2, 2)].reshape(WIDE, DIM)
            logits = dot_rows(q_far[rows, :], key_tile)
            top, total, weights, out = weigh(logits, value_tile)
            weights_far[d, rows, :] = weights
            top_far[d, rows, :] = jnp.broadcast_to(top, (CHUNK, 128))
            total_far[d, local, :] = total
            out_far[d, local, :] = out
            return carry

        lax.fori_loop(0, HALF // 2, step, 0)
        top = top_far[0, rows, :]
        for d in range(1, HALF // 2):
            top = jnp.maximum(top, top_far[d, rows, :])
        total = jnp.zeros((CHUNK, 128), jnp.float32)
        out = jnp.zeros((CHUNK, 128), jnp.float32)
        for d in range(HALF // 2):
            factor = jnp.exp2((top_far[d, rows, :] - top) * SCALE)
            total = total + factor * total_far[d]
            out = out + factor * out_far[d]
        total = jnp.sum(total, axis=1, keepdims=True)
        out = out * (1.0 / total)
        send_far[pl.ds(ci * GROUPS, GROUPS)] = out.reshape(GROUPS, GROUP, DIM).astype(jnp.bfloat16)
        low, high = to_lanes(top * SCALE + jnp.log2(total))
        stat_far[ci, :, :128] = low
        stat_far[ci, :, 128:] = high

        def start(g, carry):
            hg = ci * GROUPS + lax.rem(z + g, GROUPS)
            far_copy(hg).start()
            far_stat_copy(hg).start()
            return carry

        lax.fori_loop(0, GROUPS, start, 0)
        peer_copy(stat_far, ci).start()

    def step(i, carry):
        @pl.when(i == 1)
        def _():
            k_wait(w_core)
            v_wait(w_core)

        @pl.when(i == 2)
        def _():
            k_wait(w_left)
            k_copy(w_left, 3, w_right).start()
            k_copy(w_left, 4, w_core).start()
            k_wait(w_right)
            k_copy(w_right, 5, w_core).start()
            v_wait(w_right)
            v_copy(w_right, 3, w_left).start()
            v_copy(w_right, 5, w_core).start()
            v_wait(w_left)
            v_copy(w_left, 4, w_core).start()

        @pl.when(i == 4)
        def _():
            for dy in (3, 1):
                k_wait(place(dy, 1))
                v_wait(place(dy, 1))

        @pl.when(i == 5)
        def _():
            far_block = place(2, 0)
            k_wait(far_block)
            k_copy(far_block, 6, w_core).start()
            v_wait(far_block)
            v_copy(far_block, 6, w_core).start()
            k_wait(place(2, 1))
            v_wait(place(2, 1))

        @pl.when(jnp.logical_and(is_early, i >= 5))
        def _():
            rectangle(lax.rem(x + i - 5, CHUNKS))

        dy = jnp.where(i == 1, 0, jnp.where(i >= 6, 2, jnp.where(lax.rem(i, 2) == 0, 3, 1)))
        flip = jnp.where(jnp.logical_or(i == 1, jnp.logical_or(i == 4, jnp.logical_or(i == 5, i == 7))), 1, 0)
        block = place(dy, flip)

        @pl.when(jnp.logical_and(i < 8, block < w))
        def _():
            triangle(block, False)

        @pl.when(i == 7)
        def _():
            settle_triangle()

        return carry

    lax.fori_loop(1, 9, step, 0)

    def add_columns(count, rows, tops, weights, lse, width):
        per = width // ROWS

        def tile(j, carry):
            factor = jnp.exp2(tops[j, rows, :] * SCALE - lse)
            for u in range(width // 128):
                part = weights[j, rows, u * 128 : (u + 1) * 128].astype(jnp.float32) * factor
                part = jnp.sum(part.reshape(CHUNK // 8, 8, 128), axis=0)
                lanes = slice(u % 6 * 128, u % 6 * 128 + 128)
                column[j * per + u // 6, :, lanes] += part
            return carry

        lax.fori_loop(0, count, tile, 0)

    def both(one, two):
        top = jnp.maximum(one, two)
        return top + jnp.log2(jnp.exp2(one - top) + jnp.exp2(two - top))

    def columns(i, carry):
        ci = lax.rem(x + i, CHUNKS)
        rows = pl.ds(pl.multiple_of(ci * CHUNK, CHUNK), CHUNK)
        peer_copy(stat_own, ci).wait_recv()

        @pl.when(is_early)
        def _():
            add_columns(w + 1, rows, top_tri, weights_tri, lse_col[rows, :], ROWS)
            lse = to_column(both(stat_far[ci], stat_peer[ci]))
            add_columns(HALF // 2, rows, top_far, weights_far, lse, WIDE)

        @pl.when(is_late)
        def _():
            lse = to_column(both(stat_own[ci], stat_peer[ci]))
            add_columns(w + 1, rows, top_tri, weights_tri, lse, ROWS)

        return carry

    lax.fori_loop(0, CHUNKS, columns, 0)
    for j in range(HALF):
        column_out[j] = jnp.sum(column[j], axis=0, keepdims=True)

    def col_copy(block):
        return copy(
            column_out.at[block], column_in.at[w], col_send.at[block], col_recv.at[w], half_device(block)
        )

    def col_start(j, carry):
        col_copy(lax.rem(w + j, HALF)).start()
        return carry

    lax.fori_loop(1, HALF, col_start, 0)
    column_in[w] = column_out[w]

    def arrived(j, carry):
        hg = lax.rem(h + j, HEADS)
        copy(send_own.at[hg], got_own.at[hg], own_send.at[hg], own_recv.at[hg], (hg, b)).wait_recv()
        return carry

    lax.fori_loop(1, HEADS, arrived, 0)

    @pl.when(is_early)
    def _():
        for hh in range(HEADS):
            att_ref[:, hh * 128 : (hh + 1) * 128] = got_own[hh]

    @pl.when(is_late)
    def _():
        def stat_arrived(j, carry):
            hg = lax.rem(h + j, HEADS)
            copy(
                stat_own.at[0], got_stat_own.at[hg], own_stat_send.at[hg], own_stat_recv.at[hg], (hg, b)
            ).wait_recv()
            return carry

        lax.fori_loop(1, HEADS, stat_arrived, 0)

        def far_arrived(j, carry):
            hg = lax.rem(h + j, HEADS)
            device = (hg, w)
            copy(send_far.at[hg], got_far.at[hg], far_send.at[hg], far_recv.at[hg], device).wait_recv()
            copy(
                stat_far.at[0], got_stat_far.at[hg], far_stat_send.at[hg], far_stat_recv.at[hg], device
            ).wait_recv()
            return carry

        lax.fori_loop(0, HEADS, far_arrived, 0)
        pad = jnp.zeros((128 - HEADS, 256), jnp.float32)
        stat_a = jnp.concatenate([got_stat_own[hh] for hh in range(HEADS)] + [pad], axis=0)
        stat_b = jnp.concatenate([got_stat_far[hh] for hh in range(HEADS)] + [pad], axis=0)
        turned_a[...] = jnp.transpose(stat_a)
        turned_b[...] = jnp.transpose(stat_b)
        mine = pl.ds(pl.multiple_of(z * GROUP, 8), GROUP)
        lse_a, lse_b = turned_a[mine, :], turned_b[mine, :]
        share_a = 1.0 / (1.0 + jnp.exp2(lse_b - lse_a))
        share_b = 1.0 / (1.0 + jnp.exp2(lse_a - lse_b))
        for hh in range(HEADS):
            merged = (
                got_own[hh].astype(jnp.float32) * share_a[:, hh : hh + 1]
                + got_far[hh].astype(jnp.float32) * share_b[:, hh : hh + 1]
            )
            att_ref[:, hh * 128 : (hh + 1) * 128] = merged.astype(jnp.bfloat16)

    def col_arrived(j, carry):
        block = lax.rem(w + j, HALF)
        copy(
            column_out.at[block], column_in.at[block], col_send.at[block], col_recv.at[block],
            half_device(block),
        ).wait_recv()
        return carry

    lax.fori_loop(1, HALF, col_arrived, 0)
    heavy = column_in[0]
    for j in range(1, HALF):
        heavy = heavy + column_in[j]
    heavy_ref[...] = heavy

    for slot in range(7):
        k_copy(w, slot, w_core).wait_send()
        v_copy(w, slot, w_core).wait_send()

    def own_left(j, carry):
        hg = lax.rem(h + j, HEADS)
        own_copy(hg).wait_send()

        @pl.when(is_late)
        def _():
            own_stat_copy(hg).wait_send()

        return carry

    lax.fori_loop(1, HEADS, own_left, 0)

    @pl.when(is_early)
    def _():
        def far_left(hg, carry):
            far_copy(hg).wait_send()
            far_stat_copy(hg).wait_send()
            return carry

        lax.fori_loop(0, HEADS, far_left, 0)

    def chunk_left(ci, carry):
        peer_copy(stat_own, ci).wait_send()

        @pl.when(is_late)
        def _():
            q_copy(ci).wait_send()

        return carry

    lax.fori_loop(0, CHUNKS, chunk_left, 0)

    def col_left(j, carry):
        col_copy(lax.rem(w + j, HALF)).wait_send()
        return carry

    lax.fori_loop(1, HALF, col_left, 0)


def local(queries, key_states, value_states):
    bf16, f32 = jnp.bfloat16, jnp.float32
    vmem, dma = pltpu.VMEM, pltpu.SemaphoreType.DMA
    whole = pl.BlockSpec(memory_space=pltpu.VMEM)
    quarter = HALF // 2
    return pl.pallas_call(
        kernel,
        out_shape=(
            jax.ShapeDtypeStruct((GROUP, HEADS * DIM), bf16),
            jax.ShapeDtypeStruct((1, ROWS), f32),
        ),
        in_specs=[whole] * 3,
        out_specs=(whole, whole),
        scratch_shapes=[
            vmem((HALF, ROWS, DIM), bf16),
            vmem((HALF, ROWS, DIM), bf16),
            vmem((ROWS, DIM), bf16),
            vmem((HALF, ROWS, ROWS), bf16),
            vmem((HALF, ROWS, 128), f32),
            vmem((HALF, ROWS, 128), f32),
            vmem((HALF, ROWS, DIM), f32),
            vmem((quarter, ROWS, WIDE), bf16),
            vmem((quarter, ROWS, 128), f32),
            vmem((quarter, CHUNK, 128), f32),
            vmem((quarter, CHUNK, DIM), f32),
            vmem((ROWS, 128), f32),
            vmem((HEADS, GROUP, DIM), bf16),
            vmem((HEADS, GROUP, DIM), bf16),
            vmem((CHUNKS, 1, 256), f32),
            vmem((CHUNKS, 1, 256), f32),
            vmem((CHUNKS, 1, 256), f32),
            vmem((HEADS, GROUP, DIM), bf16),
            vmem((HEADS, GROUP, DIM), bf16),
            vmem((HEADS, 1, 256), f32),
            vmem((HEADS, 1, 256), f32),
            vmem((256, 128), f32),
            vmem((256, 128), f32),
            vmem((HALF, 8, ROWS), f32),
            vmem((HALF, 1, ROWS), f32),
            vmem((HALF, 1, ROWS), f32),
            dma((7,)), dma((HALF,)), dma((7,)), dma((HALF,)), dma((CHUNKS,)), dma((CHUNKS,)),
            dma((HEADS,)), dma((HEADS,)), dma((HEADS,)), dma((HEADS,)),
            dma((HEADS,)), dma((HEADS,)), dma((HEADS,)), dma((HEADS,)),
            dma((CHUNKS,)), dma((CHUNKS,)), dma((HALF,)), dma((HALF,)),
        ],
        compiler_params=pltpu.CompilerParams(
            collective_id=0, has_side_effects=True, vmem_limit_bytes=58 * 1024 * 1024
        ),
    )(queries, key_states, value_states)


def solution(mesh):
    placed = (P("blk", "head"), P("blk", "head"), P("blk", "head"))
    return jax.shard_map(
        local,
        mesh=mesh,
        in_specs=placed,
        out_specs=(P(("blk", "head"), None), P("head", "blk")),
        check_vma=False,
    )
```

```python
import functools
import math

import jax
import jax.numpy as jnp
from jax import lax
from jax.experimental import pallas as pl
from jax.experimental.pallas import tpu as pltpu
from jax.sharding import PartitionSpec as P

MESH = pl.DeviceIdType.MESH
DIM = 128
ROWS = 768
HEADS = 32
HALF = 8
CHUNK = 192
CHUNKS = ROWS // CHUNK
GROUP = ROWS // HEADS
GROUPS = CHUNK // GROUP
TILE = 384
WIDE = 1536
SCALE = math.log2(math.e) / math.sqrt(DIM)
LOW = -1e30


def dot_rows(a, b):
    return lax.dot_general(a, b, (((1,), (1,)), ((), ())), preferred_element_type=jnp.float32)


def dot(a, b):
    return lax.dot_general(a, b, (((1,), (0,)), ((), ())), preferred_element_type=jnp.float32)


def fold_lanes(value, op):
    out = value[:, :128]
    for u in range(1, value.shape[1] // 128):
        out = op(out, value[:, u * 128 : (u + 1) * 128])
    return out


def weigh(logits, values):
    top = jnp.max(fold_lanes(logits, jnp.maximum), axis=1, keepdims=True)
    expo = jnp.exp2((logits - top) * SCALE)
    total = fold_lanes(expo, jnp.add)
    weights = expo.astype(jnp.bfloat16)
    return top, total, weights, dot(weights, values)


def to_lanes(column):
    out = []
    for begin, size in ((0, 128), (128, 64)):
        part = column[begin : begin + size]
        row = lax.broadcasted_iota(jnp.int32, part.shape, 0)
        lane = lax.broadcasted_iota(jnp.int32, part.shape, 1)
        out.append(jnp.sum(jnp.where(row == lane, part, 0.0), axis=0, keepdims=True))
    return out


def to_groups(column):
    parts = column.reshape(GROUPS, GROUP, 128)
    row = lax.broadcasted_iota(jnp.int32, parts.shape, 1)
    lane = lax.broadcasted_iota(jnp.int32, parts.shape, 2)
    return jnp.sum(jnp.where(row == lane, parts, 0.0), axis=1, keepdims=True)


def to_column(row):
    parts = []
    for begin, size in ((0, 128), (128, 64)):
        square = jnp.broadcast_to(row[:, begin : begin + 128], (128, 128))
        parts.append(jnp.transpose(square)[:size])
    return jnp.concatenate(parts, axis=0)


def kernel(
    q_ref, k_ref, v_ref, att_ref, heavy_ref,
    keys, values, q_far, weights_tri, top_tri, total_tri, out_tri,
    weights_far, top_far, total_far, out_far, lse_col,
    send_own, send_far, stat_own, stat_far, stat_peer,
    tag_own, tag_far, got_own, got_far, got_stat_own, got_stat_far,
    column, column_out, column_in,
    k_send, k_recv, v_send, v_recv, q_send, q_recv,
    own_send, own_recv, own_stat_send, own_stat_recv,
    far_send, far_recv, far_stat_send, far_stat_recv,
    peer_send, peer_recv, col_send, col_recv, ready,
):
    h = lax.axis_index("head")
    b = lax.axis_index("blk")
    later = b // HALF
    w = lax.rem(b, HALF)
    y, core = w // 2, lax.rem(w, 2)
    x, z = h // 8, lax.rem(h, 8)
    base = later * HALF
    is_early, is_late = later == 0, later == 1

    def place(dy, flip):
        yy = lax.rem(y + dy, 4)
        return yy * 2 + (lax.rem(core + flip, 2))

    def half_device(block):
        return (h, base + block)

    partner = (h, w + (1 - later) * HALF)
    w_right, w_left, w_core = place(1, 0), place(3, 0), place(0, 1)

    def copy(src, dst, send_sem, recv_sem, device):
        return pltpu.make_async_remote_copy(
            src_ref=src, dst_ref=dst, send_sem=send_sem, recv_sem=recv_sem,
            device_id=device, device_id_type=MESH,
        )

    barrier = pltpu.get_barrier_semaphore()

    def greet(device):
        pl.semaphore_signal(barrier, inc=1, device_id=device, device_id_type=MESH)

    def along_z(step):
        return ((z >= step, (h - step, b)), (z + step < 8, (h + step, b)))

    def along_x():
        return [(lax.rem(h + 8 * d, HEADS), b) for d in (1, 2, 3)]

    def count_z(step):
        return (z >= step).astype(jnp.int32) + (z + step < 8).astype(jnp.int32)

    for exists, device in along_z(1):
        pl.when(exists)(functools.partial(greet, device))
    for device in along_x():
        greet(device)
    for block in (w_right, w_left, w_core):
        greet(half_device(block))
    pl.when(is_early)(functools.partial(greet, partner))

    def tell(index, device):
        pl.semaphore_signal(ready.at[index], inc=1, device_id=device, device_id_type=MESH)

    def tell_z(index, step):
        for exists, device in along_z(step):
            pl.when(exists)(functools.partial(tell, index, device))

    def hear(index, count):
        pl.semaphore_wait(ready.at[index], count)

    keys[w] = k_ref[...]
    values[w] = v_ref[...]

    def triangle(block, masked, tiles):
        for t in tiles:
            rows = pl.ds(t * TILE, TILE)
            logits = dot_rows(q_ref[rows, :], keys[block])
            if masked:
                row = lax.broadcasted_iota(jnp.int32, logits.shape, 0) + t * TILE
                col = lax.broadcasted_iota(jnp.int32, logits.shape, 1)
                logits = jnp.where(col <= row, logits, LOW)
            top, total, weights, out = weigh(logits, values[block])
            weights_tri[block, rows, :] = weights
            top_tri[block, rows, :] = jnp.broadcast_to(top, (TILE, 128))
            total_tri[block, rows, :] = total
            out_tri[block, rows, :] = out

    pl.semaphore_wait(barrier, 6 + count_z(1) + later)

    def q_copy(ci):
        rows = pl.ds(pl.multiple_of(ci * CHUNK, CHUNK), CHUNK)
        return copy(q_ref.at[rows], q_far.at[rows], q_send.at[ci], q_recv.at[ci], partner)

    @pl.when(is_late)
    def _():
        def start(i, carry):
            q_copy(lax.rem(x + i, CHUNKS)).start()
            return carry

        lax.fori_loop(0, CHUNKS, start, 0)

    def k_copy(block, slot, to):
        return copy(keys.at[block], keys.at[block], k_send.at[slot], k_recv.at[block], half_device(to))

    def v_copy(block, slot, to):
        return copy(values.at[block], values.at[block], v_send.at[slot], v_recv.at[block], half_device(to))

    k_copy(w, 0, w_right).start()
    k_copy(w, 1, w_left).start()
    k_copy(w, 2, w_core).start()
    v_copy(w, 0, w_right).start()
    v_copy(w, 1, w_left).start()
    v_copy(w, 2, w_core).start()

    tell_z(0, 1)
    triangle(w, True, (0,))
    hear(0, count_z(1))
    tell_z(1, 2)
    triangle(w, True, (1,))
    hear(1, count_z(2))
    tell_z(2, 4)
    column[...] = jnp.zeros_like(column)

    def k_wait(block):
        k_copy(block, 0, w_core).wait_recv()

    def v_wait(block):
        v_copy(block, 0, w_core).wait_recv()

    def own_copy(hg):
        return copy(send_own.at[hg], got_own.at[h], own_send.at[0], own_recv.at[0], (hg, b))

    def own_stat_copy(hg):
        return copy(
            tag_own.at[hg], got_stat_own.at[h],
            own_stat_send.at[0], own_stat_recv.at[0], (hg, b),
        )

    def far_copy(hg):
        return copy(send_far.at[hg], got_far.at[h], far_send.at[0], far_recv.at[0], (hg, w + HALF))

    def far_stat_copy(hg):
        return copy(
            tag_far.at[hg], got_stat_far.at[h],
            far_stat_send.at[0], far_stat_recv.at[0], (hg, w + HALF),
        )

    def peer_copy(stat, ci):
        return copy(stat.at[ci], stat_peer.at[ci], peer_send.at[ci], peer_recv.at[ci], partner)

    def settle(count, rows, tops, totals, outs):
        top = lax.fori_loop(
            1, count, lambda j, top: jnp.maximum(top, tops[j, rows, :]), tops[0, rows, :]
        )

        def add(j, carry):
            total, out = carry
            factor = jnp.exp2((tops[j, rows, :] - top) * SCALE)
            return (total + factor * totals[j, rows, :], out + factor * outs[j, rows, :])

        zero = jnp.zeros((CHUNK, 128), jnp.float32)
        total, out = lax.fori_loop(0, count, add, (zero, zero))
        total = jnp.sum(total, axis=1, keepdims=True)
        return out * (1.0 / total), top * SCALE + jnp.log2(total)

    def settle_triangle():
        def chunk(ci, carry):
            rows = pl.ds(pl.multiple_of(ci * CHUNK, CHUNK), CHUNK)
            out, lse = settle(w + 1, rows, top_tri, total_tri, out_tri)
            send_own[pl.ds(ci * GROUPS, GROUPS)] = out.reshape(GROUPS, GROUP, DIM).astype(jnp.bfloat16)
            lse_col[rows, :] = lse
            tag_own[pl.ds(ci * GROUPS, GROUPS)] = to_groups(lse)
            low, high = to_lanes(lse)
            stat_own[ci, :, :128] = low
            stat_own[ci, :, 128:] = high
            return carry

        lax.fori_loop(0, CHUNKS, chunk, 0)

        @pl.when(is_late)
        def _():
            for ci in range(CHUNKS):
                peer_copy(stat_own, ci).start()

        got_own[h] = send_own[h]

        def start(j, carry):
            hg = lax.rem(h + j, HEADS)
            own_copy(hg).start()

            @pl.when(is_late)
            def _():
                own_stat_copy(hg).start()

            return carry

        lax.fori_loop(1, HEADS, start, 0)

        @pl.when(is_late)
        def _():
            got_stat_own[h] = tag_own[h]

    def rectangle(ci):
        q_copy(ci).wait_recv()
        rows = pl.ds(pl.multiple_of(ci * CHUNK, CHUNK), CHUNK)
        local = pl.ds(0, CHUNK)

        def step(d, carry):
            key_tile = keys[pl.ds(d * 2, 2)].reshape(WIDE, DIM)
            value_tile = values[pl.ds(d * 2, 2)].reshape(WIDE, DIM)
            logits = dot_rows(q_far[rows, :], key_tile)
            top, total, weights, out = weigh(logits, value_tile)
            weights_far[d, rows, :] = weights
            top_far[d, rows, :] = jnp.broadcast_to(top, (CHUNK, 128))
            total_far[d, local, :] = total
            out_far[d, local, :] = out
            return carry

        lax.fori_loop(0, HALF // 2, step, 0, unroll=2)
        top = top_far[0, rows, :]
        for d in range(1, HALF // 2):
            top = jnp.maximum(top, top_far[d, rows, :])
        total = jnp.zeros((CHUNK, 128), jnp.float32)
        out = jnp.zeros((CHUNK, 128), jnp.float32)
        for d in range(HALF // 2):
            factor = jnp.exp2((top_far[d, rows, :] - top) * SCALE)
            total = total + factor * total_far[d]
            out = out + factor * out_far[d]
        total = jnp.sum(total, axis=1, keepdims=True)
        out = out * (1.0 / total)
        send_far[pl.ds(ci * GROUPS, GROUPS)] = out.reshape(GROUPS, GROUP, DIM).astype(jnp.bfloat16)
        lse = top * SCALE + jnp.log2(total)
        tag_far[pl.ds(ci * GROUPS, GROUPS)] = to_groups(lse)
        low, high = to_lanes(lse)
        stat_far[ci, :, :128] = low
        stat_far[ci, :, 128:] = high

        def start(g, carry):
            hg = ci * GROUPS + lax.rem(z + g, GROUPS)
            far_copy(hg).start()
            far_stat_copy(hg).start()
            return carry

        lax.fori_loop(0, GROUPS, start, 0)
        peer_copy(stat_far, ci).start()

    def step(i, carry):
        @pl.when(i == 1)
        def _():
            k_wait(w_core)
            v_wait(w_core)

        @pl.when(i == 2)
        def _():
            hear(2, count_z(4))
            for device in along_x():
                tell(3, device)
            hear(3, 3)
            pl.when(is_late)(functools.partial(tell, 4, partner))
            k_wait(w_left)
            k_copy(w_left, 3, w_right).start()
            k_copy(w_left, 4, w_core).start()
            k_wait(w_right)
            k_copy(w_right, 5, w_core).start()
            v_wait(w_right)
            v_copy(w_right, 3, w_left).start()
            v_copy(w_right, 5, w_core).start()
            v_wait(w_left)
            v_copy(w_left, 4, w_core).start()

        @pl.when(i == 4)
        def _():
            for dy in (3, 1):
                k_wait(place(dy, 1))
                v_wait(place(dy, 1))

        @pl.when(i == 5)
        def _():
            far_block = place(2, 0)
            k_wait(far_block)
            k_copy(far_block, 6, w_core).start()
            v_wait(far_block)
            v_copy(far_block, 6, w_core).start()
            k_wait(place(2, 1))
            v_wait(place(2, 1))
            pl.when(is_early)(functools.partial(hear, 4, 1))

        @pl.when(jnp.logical_and(is_early, i >= 5))
        def _():
            rectangle(lax.rem(x + i - 5, CHUNKS))

        dy = jnp.where(i == 1, 0, jnp.where(i >= 6, 2, jnp.where(lax.rem(i, 2) == 0, 3, 1)))
        flip = jnp.where(jnp.logical_or(i == 1, jnp.logical_or(i == 4, jnp.logical_or(i == 5, i == 7))), 1, 0)
        block = place(dy, flip)

        @pl.when(jnp.logical_and(i < 8, block < w))
        def _():
            triangle(block, False, range(ROWS // TILE))

        @pl.when(i == 7)
        def _():
            settle_triangle()

        return carry

    lax.fori_loop(1, 9, step, 0)

    def add_columns(count, rows, tops, weights, lse, width):
        per = width // ROWS

        def tile(j, carry):
            factor = jnp.exp2(tops[j, rows, :] * SCALE - lse)
            for u in range(width // 128):
                part = weights[j, rows, u * 128 : (u + 1) * 128].astype(jnp.float32) * factor
                part = jnp.sum(part.reshape(CHUNK // 8, 8, 128), axis=0)
                lanes = slice(u % 6 * 128, u % 6 * 128 + 128)
                column[j * per + u // 6, :, lanes] += part
            return carry

        lax.fori_loop(0, count, tile, 0)

    def both(one, two):
        top = jnp.maximum(one, two)
        return top + jnp.log2(jnp.exp2(one - top) + jnp.exp2(two - top))

    def columns(i, carry):
        ci = lax.rem(x + i, CHUNKS)
        rows = pl.ds(pl.multiple_of(ci * CHUNK, CHUNK), CHUNK)
        peer_copy(stat_own, ci).wait_recv()

        @pl.when(is_early)
        def _():
            add_columns(w + 1, rows, top_tri, weights_tri, lse_col[rows, :], ROWS)
            lse = to_column(both(stat_far[ci], stat_peer[ci]))
            add_columns(HALF // 2, rows, top_far, weights_far, lse, WIDE)

        @pl.when(is_late)
        def _():
            lse = to_column(both(stat_own[ci], stat_peer[ci]))
            add_columns(w + 1, rows, top_tri, weights_tri, lse, ROWS)

        return carry

    lax.fori_loop(0, CHUNKS, columns, 0)
    for j in range(HALF):
        column_out[j] = jnp.sum(column[j], axis=0, keepdims=True)

    def col_copy(block):
        return copy(
            column_out.at[block], column_in.at[w], col_send.at[block], col_recv.at[w], half_device(block)
        )

    def col_start(j, carry):
        col_copy(lax.rem(w + j, HALF)).start()
        return carry

    lax.fori_loop(1, HALF, col_start, 0)
    column_in[w] = column_out[w]

    others, everyone = pl.ds(0, HEADS - 1), pl.ds(0, HEADS)

    def all_own(which):
        return copy(
            send_own.at[which], got_own.at[which], own_send.at[0], own_recv.at[0], half_device(w_core)
        )

    def all_own_stat(which):
        return copy(
            tag_own.at[which], got_stat_own.at[which],
            own_stat_send.at[0], own_stat_recv.at[0], half_device(w_core),
        )

    def all_far(which):
        return copy(
            send_far.at[which], got_far.at[which], far_send.at[0], far_recv.at[0], partner
        )

    def all_far_stat(which):
        return copy(
            tag_far.at[which], got_stat_far.at[which],
            far_stat_send.at[0], far_stat_recv.at[0], partner,
        )

    all_own(others).wait_recv()

    @pl.when(is_early)
    def _():
        for hh in range(HEADS):
            att_ref[:, hh * 128 : (hh + 1) * 128] = got_own[hh]

    @pl.when(is_late)
    def _():
        all_own_stat(others).wait_recv()
        all_far(everyone).wait_recv()
        all_far_stat(everyone).wait_recv()
        pad = jnp.zeros((128 - HEADS, 128), jnp.float32)
        stat_a = jnp.concatenate([got_stat_own[hh] for hh in range(HEADS)] + [pad], axis=0)
        stat_b = jnp.concatenate([got_stat_far[hh] for hh in range(HEADS)] + [pad], axis=0)
        lse_a = jnp.transpose(stat_a)[:GROUP]
        lse_b = jnp.transpose(stat_b)[:GROUP]
        share_a = 1.0 / (1.0 + jnp.exp2(lse_b - lse_a))
        share_b = 1.0 / (1.0 + jnp.exp2(lse_a - lse_b))
        for hh in range(HEADS):
            merged = (
                got_own[hh].astype(jnp.float32) * share_a[:, hh : hh + 1]
                + got_far[hh].astype(jnp.float32) * share_b[:, hh : hh + 1]
            )
            att_ref[:, hh * 128 : (hh + 1) * 128] = merged.astype(jnp.bfloat16)

    def col_arrived(j, carry):
        block = lax.rem(w + j, HALF)
        copy(
            column_out.at[block], column_in.at[block], col_send.at[block], col_recv.at[block],
            half_device(block),
        ).wait_recv()
        return carry

    lax.fori_loop(1, HALF, col_arrived, 0)
    heavy = column_in[0]
    for j in range(1, HALF):
        heavy = heavy + column_in[j]
    heavy_ref[...] = heavy

    for slot in range(7):
        k_copy(w, slot, w_core).wait_send()
        v_copy(w, slot, w_core).wait_send()

    all_own(others).wait_send()

    @pl.when(is_late)
    def _():
        all_own_stat(others).wait_send()

    @pl.when(is_early)
    def _():
        all_far(everyone).wait_send()
        all_far_stat(everyone).wait_send()

    def chunk_left(ci, carry):
        peer_copy(stat_own, ci).wait_send()

        @pl.when(is_late)
        def _():
            q_copy(ci).wait_send()

        return carry

    lax.fori_loop(0, CHUNKS, chunk_left, 0)

    def col_left(j, carry):
        col_copy(lax.rem(w + j, HALF)).wait_send()
        return carry

    lax.fori_loop(1, HALF, col_left, 0)


def local(queries, key_states, value_states):
    bf16, f32 = jnp.bfloat16, jnp.float32
    vmem, dma = pltpu.VMEM, pltpu.SemaphoreType.DMA
    whole = pl.BlockSpec(memory_space=pltpu.VMEM)
    quarter = HALF // 2
    return pl.pallas_call(
        kernel,
        out_shape=(
            jax.ShapeDtypeStruct((GROUP, HEADS * DIM), bf16),
            jax.ShapeDtypeStruct((1, ROWS), f32),
        ),
        in_specs=[whole] * 3,
        out_specs=(whole, whole),
        scratch_shapes=[
            vmem((HALF, ROWS, DIM), bf16),
            vmem((HALF, ROWS, DIM), bf16),
            vmem((ROWS, DIM), bf16),
            vmem((HALF, ROWS, ROWS), bf16),
            vmem((HALF, ROWS, 128), f32),
            vmem((HALF, ROWS, 128), f32),
            vmem((HALF, ROWS, DIM), f32),
            vmem((quarter, ROWS, WIDE), bf16),
            vmem((quarter, ROWS, 128), f32),
            vmem((quarter, CHUNK, 128), f32),
            vmem((quarter, CHUNK, DIM), f32),
            vmem((ROWS, 128), f32),
            vmem((HEADS, GROUP, DIM), bf16),
            vmem((HEADS, GROUP, DIM), bf16),
            vmem((CHUNKS, 1, 256), f32),
            vmem((CHUNKS, 1, 256), f32),
            vmem((CHUNKS, 1, 256), f32),
            vmem((HEADS, 1, 128), f32),
            vmem((HEADS, 1, 128), f32),
            vmem((HEADS, GROUP, DIM), bf16),
            vmem((HEADS, GROUP, DIM), bf16),
            vmem((HEADS, 1, 128), f32),
            vmem((HEADS, 1, 128), f32),
            vmem((HALF, 8, ROWS), f32),
            vmem((HALF, 1, ROWS), f32),
            vmem((HALF, 1, ROWS), f32),
            dma((7,)), dma((HALF,)), dma((7,)), dma((HALF,)), dma((CHUNKS,)), dma((CHUNKS,)),
            dma((1,)), dma((1,)), dma((1,)), dma((1,)),
            dma((1,)), dma((1,)), dma((1,)), dma((1,)),
            dma((CHUNKS,)), dma((CHUNKS,)), dma((HALF,)), dma((HALF,)),
            pltpu.SemaphoreType.REGULAR((5,)),
        ],
        compiler_params=pltpu.CompilerParams(
            collective_id=0, has_side_effects=True, vmem_limit_bytes=58 * 1024 * 1024
        ),
    )(queries, key_states, value_states)


def solution(mesh):
    placed = (P("blk", "head"), P("blk", "head"), P("blk", "head"))
    return jax.shard_map(
        local,
        mesh=mesh,
        in_specs=placed,
        out_specs=(P(("blk", "head"), None), P("head", "blk")),
        check_vma=False,
    )
```

```python
import functools
import math

import jax
import jax.numpy as jnp
from jax import lax
from jax.experimental import pallas as pl
from jax.experimental.pallas import tpu as pltpu
from jax.sharding import PartitionSpec as P

MESH = pl.DeviceIdType.MESH
DIM = 128
ROWS = 768
HEADS = 32
HALF = 8
CHUNK = 192
CHUNKS = ROWS // CHUNK
GROUP = ROWS // HEADS
GROUPS = CHUNK // GROUP
TILE = 384
WIDE = 1536
SCALE = math.log2(math.e) / math.sqrt(DIM)
LOW = -1e30


def dot_rows(a, b):
    return lax.dot_general(a, b, (((1,), (1,)), ((), ())), preferred_element_type=jnp.float32)


def dot(a, b):
    return lax.dot_general(a, b, (((1,), (0,)), ((), ())), preferred_element_type=jnp.float32)


def fold_lanes(value, op):
    out = value[:, :128]
    for u in range(1, value.shape[1] // 128):
        out = op(out, value[:, u * 128 : (u + 1) * 128])
    return out


def weigh(logits, values):
    top = jnp.max(fold_lanes(logits, jnp.maximum), axis=1, keepdims=True)
    expo = jnp.exp2((logits - top) * SCALE)
    total = fold_lanes(expo, jnp.add)
    weights = expo.astype(jnp.bfloat16)
    return top, total, weights, dot(weights, values)


def to_lanes(column):
    out = []
    for begin, size in ((0, 128), (128, 64)):
        part = column[begin : begin + size]
        row = lax.broadcasted_iota(jnp.int32, part.shape, 0)
        lane = lax.broadcasted_iota(jnp.int32, part.shape, 1)
        out.append(jnp.sum(jnp.where(row == lane, part, 0.0), axis=0, keepdims=True))
    return out


def to_groups(column):
    parts = column.reshape(GROUPS, GROUP, 128)
    row = lax.broadcasted_iota(jnp.int32, parts.shape, 1)
    lane = lax.broadcasted_iota(jnp.int32, parts.shape, 2)
    return jnp.sum(jnp.where(row == lane, parts, 0.0), axis=1, keepdims=True)


def to_column(row):
    parts = []
    for begin, size in ((0, 128), (128, 64)):
        square = jnp.broadcast_to(row[:, begin : begin + 128], (128, 128))
        parts.append(jnp.transpose(square)[:size])
    return jnp.concatenate(parts, axis=0)


def kernel(
    q_ref, k_ref, v_ref, att_ref, heavy_ref,
    keys, values, q_far, weights_tri, top_tri, total_tri, out_tri,
    weights_far, top_far, total_far, out_far, lse_col,
    send_own, send_far, stat_own, stat_far, stat_peer,
    tag_own, tag_far, got_own, got_far, got_stat_own, got_stat_far,
    column, column_out, column_in,
    k_send, k_recv, v_send, v_recv, q_send, q_recv,
    own_send, own_recv, own_stat_send, own_stat_recv,
    far_send, far_recv, far_stat_send, far_stat_recv,
    peer_send, peer_recv, col_send, col_recv, ready,
):
    h = lax.axis_index("head")
    b = lax.axis_index("blk")
    later = b // HALF
    w = lax.rem(b, HALF)
    y, core = w // 2, lax.rem(w, 2)
    x, z = h // 8, lax.rem(h, 8)
    base = later * HALF
    is_early, is_late = later == 0, later == 1

    def place(dy, flip):
        yy = lax.rem(y + dy, 4)
        return yy * 2 + (lax.rem(core + flip, 2))

    def half_device(block):
        return (h, base + block)

    partner = (h, w + (1 - later) * HALF)
    w_right, w_left, w_core = place(1, 0), place(3, 0), place(0, 1)

    def copy(src, dst, send_sem, recv_sem, device):
        return pltpu.make_async_remote_copy(
            src_ref=src, dst_ref=dst, send_sem=send_sem, recv_sem=recv_sem,
            device_id=device, device_id_type=MESH,
        )

    barrier = pltpu.get_barrier_semaphore()

    def greet(device):
        pl.semaphore_signal(barrier, inc=1, device_id=device, device_id_type=MESH)

    def along_z(step):
        return ((z >= step, (h - step, b)), (z + step < 8, (h + step, b)))

    def along_x():
        return [(lax.rem(h + 8 * d, HEADS), b) for d in (1, 2, 3)]

    def count_z(step):
        return (z >= step).astype(jnp.int32) + (z + step < 8).astype(jnp.int32)

    for exists, device in along_z(1):
        pl.when(exists)(functools.partial(greet, device))
    for device in along_x():
        greet(device)
    for block in (w_right, w_left, w_core):
        greet(half_device(block))
    pl.when(is_early)(functools.partial(greet, partner))

    def tell(index, device):
        pl.semaphore_signal(ready.at[index], inc=1, device_id=device, device_id_type=MESH)

    def tell_z(index, step):
        for exists, device in along_z(step):
            pl.when(exists)(functools.partial(tell, index, device))

    def hear(index, count):
        pl.semaphore_wait(ready.at[index], count)

    keys[w] = k_ref[...]
    values[w] = v_ref[...]

    def triangle(block, masked, tiles):
        for t in tiles:
            rows = pl.ds(t * TILE, TILE)
            logits = dot_rows(q_ref[rows, :], keys[block])
            if masked:
                row = lax.broadcasted_iota(jnp.int32, logits.shape, 0) + t * TILE
                col = lax.broadcasted_iota(jnp.int32, logits.shape, 1)
                logits = jnp.where(col <= row, logits, LOW)
            top, total, weights, out = weigh(logits, values[block])
            weights_tri[block, rows, :] = weights
            top_tri[block, rows, :] = jnp.broadcast_to(top, (TILE, 128))
            total_tri[block, rows, :] = total
            out_tri[block, rows, :] = out

    pl.semaphore_wait(barrier, 6 + count_z(1) + later)

    def q_copy(ci):
        rows = pl.ds(pl.multiple_of(ci * CHUNK, CHUNK), CHUNK)
        return copy(q_ref.at[rows], q_far.at[rows], q_send.at[ci], q_recv.at[ci], partner)

    def send_queries(i):
        pl.when(is_late)(lambda: q_copy(lax.rem(x + i, CHUNKS)).start())

    send_queries(0)

    def k_copy(block, slot, to):
        return copy(keys.at[block], keys.at[block], k_send.at[slot], k_recv.at[block], half_device(to))

    def v_copy(block, slot, to):
        return copy(values.at[block], values.at[block], v_send.at[slot], v_recv.at[block], half_device(to))

    k_copy(w, 0, w_right).start()
    k_copy(w, 1, w_left).start()
    k_copy(w, 2, w_core).start()
    v_copy(w, 0, w_right).start()
    v_copy(w, 1, w_left).start()
    v_copy(w, 2, w_core).start()

    tell_z(0, 1)
    triangle(w, True, (0,))
    hear(0, count_z(1))
    tell_z(1, 2)
    triangle(w, True, (1,))
    hear(1, count_z(2))
    tell_z(2, 4)
    send_queries(1)
    column[...] = jnp.zeros_like(column)

    def k_wait(block):
        k_copy(block, 0, w_core).wait_recv()

    def v_wait(block):
        v_copy(block, 0, w_core).wait_recv()

    def own_copy(hg):
        return copy(send_own.at[hg], got_own.at[h], own_send.at[0], own_recv.at[0], (hg, b))

    def own_stat_copy(hg):
        return copy(
            tag_own.at[hg], got_stat_own.at[h],
            own_stat_send.at[0], own_stat_recv.at[0], (hg, b),
        )

    def far_copy(hg):
        return copy(send_far.at[hg], got_far.at[h], far_send.at[0], far_recv.at[0], (hg, w + HALF))

    def far_stat_copy(hg):
        return copy(
            tag_far.at[hg], got_stat_far.at[h],
            far_stat_send.at[0], far_stat_recv.at[0], (hg, w + HALF),
        )

    def peer_copy(stat, ci):
        return copy(stat.at[ci], stat_peer.at[ci], peer_send.at[ci], peer_recv.at[ci], partner)

    def settle(count, rows, tops, totals, outs):
        top = lax.fori_loop(
            1, count, lambda j, top: jnp.maximum(top, tops[j, rows, :]), tops[0, rows, :]
        )

        def add(j, carry):
            total, out = carry
            factor = jnp.exp2((tops[j, rows, :] - top) * SCALE)
            return (total + factor * totals[j, rows, :], out + factor * outs[j, rows, :])

        zero = jnp.zeros((CHUNK, 128), jnp.float32)
        total, out = lax.fori_loop(0, count, add, (zero, zero))
        total = jnp.sum(total, axis=1, keepdims=True)
        return out * (1.0 / total), top * SCALE + jnp.log2(total)

    def settle_triangle():
        def chunk(ci, carry):
            rows = pl.ds(pl.multiple_of(ci * CHUNK, CHUNK), CHUNK)
            out, lse = settle(w + 1, rows, top_tri, total_tri, out_tri)
            send_own[pl.ds(ci * GROUPS, GROUPS)] = out.reshape(GROUPS, GROUP, DIM).astype(jnp.bfloat16)
            lse_col[rows, :] = lse
            tag_own[pl.ds(ci * GROUPS, GROUPS)] = to_groups(lse)
            low, high = to_lanes(lse)
            stat_own[ci, :, :128] = low
            stat_own[ci, :, 128:] = high
            return carry

        lax.fori_loop(0, CHUNKS, chunk, 0)

        @pl.when(is_late)
        def _():
            for ci in range(CHUNKS):
                peer_copy(stat_own, ci).start()

        got_own[h] = send_own[h]

        def start(j, carry):
            hg = lax.rem(h + j, HEADS)
            own_copy(hg).start()

            @pl.when(is_late)
            def _():
                own_stat_copy(hg).start()

            return carry

        lax.fori_loop(1, HEADS, start, 0)

        @pl.when(is_late)
        def _():
            got_stat_own[h] = tag_own[h]

    def rectangle(ci, first):
        q_copy(ci).wait_recv()
        rows = pl.ds(pl.multiple_of(ci * CHUNK, CHUNK), CHUNK)
        local = pl.ds(0, CHUNK)

        def step(d, carry):
            key_tile = keys[pl.ds(d * 2, 2)].reshape(WIDE, DIM)
            value_tile = values[pl.ds(d * 2, 2)].reshape(WIDE, DIM)
            logits = dot_rows(q_far[rows, :], key_tile)
            top, total, weights, out = weigh(logits, value_tile)
            weights_far[d, rows, :] = weights
            top_far[d, rows, :] = jnp.broadcast_to(top, (CHUNK, 128))
            total_far[d, local, :] = total
            out_far[d, local, :] = out
            return carry

        lax.fori_loop(0, HALF // 2, step, 0, unroll=2)
        top = top_far[0, rows, :]
        for d in range(1, HALF // 2):
            top = jnp.maximum(top, top_far[d, rows, :])
        total = jnp.zeros((CHUNK, 128), jnp.float32)
        out = jnp.zeros((CHUNK, 128), jnp.float32)
        for d in range(HALF // 2):
            factor = jnp.exp2((top_far[d, rows, :] - top) * SCALE)
            total = total + factor * total_far[d]
            out = out + factor * out_far[d]
        total = jnp.sum(total, axis=1, keepdims=True)
        out = out * (1.0 / total)
        send_far[pl.ds(ci * GROUPS, GROUPS)] = out.reshape(GROUPS, GROUP, DIM).astype(jnp.bfloat16)
        lse = top * SCALE + jnp.log2(total)
        tag_far[pl.ds(ci * GROUPS, GROUPS)] = to_groups(lse)
        low, high = to_lanes(lse)
        stat_far[ci, :, :128] = low
        stat_far[ci, :, 128:] = high

        pl.when(first)(functools.partial(hear, 4, 1))

        def start(g, carry):
            hg = ci * GROUPS + lax.rem(z + g, GROUPS)
            far_copy(hg).start()
            far_stat_copy(hg).start()
            return carry

        lax.fori_loop(0, GROUPS, start, 0)
        peer_copy(stat_far, ci).start()

    def step(i, carry):
        @pl.when(i == 1)
        def _():
            k_wait(w_core)
            v_wait(w_core)

        @pl.when(i == 2)
        def _():
            hear(2, count_z(4))
            for device in along_x():
                tell(3, device)
            hear(3, 3)
            pl.when(is_late)(functools.partial(tell, 4, partner))
            send_queries(2)
            k_wait(w_left)
            k_copy(w_left, 3, w_right).start()
            k_copy(w_left, 4, w_core).start()
            k_wait(w_right)
            k_copy(w_right, 5, w_core).start()
            v_wait(w_right)
            v_copy(w_right, 3, w_left).start()
            v_copy(w_right, 5, w_core).start()
            v_wait(w_left)
            v_copy(w_left, 4, w_core).start()

        @pl.when(i == 4)
        def _():
            send_queries(3)
            for dy in (3, 1):
                k_wait(place(dy, 1))
                v_wait(place(dy, 1))

        @pl.when(i == 6)
        def _():
            far_block = place(2, 0)
            k_wait(far_block)
            k_copy(far_block, 6, w_core).start()
            v_wait(far_block)
            v_copy(far_block, 6, w_core).start()
            k_wait(place(2, 1))
            v_wait(place(2, 1))

        @pl.when(jnp.logical_and(is_early, i >= 6))
        def _():
            rectangle(lax.rem(x + i - 6, CHUNKS), i == 6)

        def unit(u, carry):
            dy = jnp.where(u == 1, 0, jnp.where(u >= 6, 2, jnp.where(lax.rem(u, 2) == 0, 3, 1)))
            flip = jnp.where(jnp.logical_or(u == 1, jnp.logical_or(u == 4, jnp.logical_or(u == 5, u == 7))), 1, 0)
            block = place(dy, flip)

            @pl.when(block < w)
            def _():
                triangle(block, False, range(ROWS // TILE))

            return carry

        first = jnp.where(i <= 5, i, 6)
        last = jnp.where(i <= 5, i + 1, jnp.where(i == 8, 8, 6))
        lax.fori_loop(first, last, unit, 0)

        @pl.when(i == 8)
        def _():
            settle_triangle()

        return carry

    lax.fori_loop(1, 10, step, 0)

    def add_columns(count, rows, tops, weights, lse, width):
        per = width // ROWS

        def tile(j, carry):
            factor = jnp.exp2(tops[j, rows, :] * SCALE - lse)
            for u in range(width // 128):
                part = weights[j, rows, u * 128 : (u + 1) * 128].astype(jnp.float32) * factor
                part = jnp.sum(part.reshape(CHUNK // 8, 8, 128), axis=0)
                lanes = slice(u % 6 * 128, u % 6 * 128 + 128)
                column[j * per + u // 6, :, lanes] += part
            return carry

        lax.fori_loop(0, count, tile, 0)

    def both(one, two):
        top = jnp.maximum(one, two)
        return top + jnp.log2(jnp.exp2(one - top) + jnp.exp2(two - top))

    def piece(i):
        ci = lax.rem(x + i, CHUNKS)
        return ci, pl.ds(pl.multiple_of(ci * CHUNK, CHUNK), CHUNK)

    @pl.when(is_early)
    def _():
        def near(i, carry):
            ci, rows = piece(i)
            add_columns(w + 1, rows, top_tri, weights_tri, lse_col[rows, :], ROWS)
            return carry

        lax.fori_loop(0, CHUNKS, near, 0)

        def distant(i, carry):
            ci, rows = piece(i)
            peer_copy(stat_own, ci).wait_recv()
            lse = to_column(both(stat_far[ci], stat_peer[ci]))
            add_columns(HALF // 2, rows, top_far, weights_far, lse, WIDE)
            return carry

        lax.fori_loop(0, CHUNKS, distant, 0)

    @pl.when(is_late)
    def _():
        def near(i, carry):
            ci, rows = piece(i)
            peer_copy(stat_own, ci).wait_recv()
            lse = to_column(both(stat_own[ci], stat_peer[ci]))
            add_columns(w + 1, rows, top_tri, weights_tri, lse, ROWS)
            return carry

        lax.fori_loop(0, CHUNKS, near, 0)

    for j in range(HALF):
        column_out[j] = jnp.sum(column[j], axis=0, keepdims=True)

    def col_copy(block):
        return copy(
            column_out.at[block], column_in.at[w], col_send.at[block], col_recv.at[w], half_device(block)
        )

    def col_start(j, carry):
        col_copy(lax.rem(w + j, HALF)).start()
        return carry

    lax.fori_loop(1, HALF, col_start, 0)
    column_in[w] = column_out[w]

    others, everyone = pl.ds(0, HEADS - 1), pl.ds(0, HEADS)

    def all_own(which):
        return copy(
            send_own.at[which], got_own.at[which], own_send.at[0], own_recv.at[0], half_device(w_core)
        )

    def all_own_stat(which):
        return copy(
            tag_own.at[which], got_stat_own.at[which],
            own_stat_send.at[0], own_stat_recv.at[0], half_device(w_core),
        )

    def all_far(which):
        return copy(
            send_far.at[which], got_far.at[which], far_send.at[0], far_recv.at[0], partner
        )

    def all_far_stat(which):
        return copy(
            tag_far.at[which], got_stat_far.at[which],
            far_stat_send.at[0], far_stat_recv.at[0], partner,
        )

    all_own(others).wait_recv()

    @pl.when(is_early)
    def _():
        for hh in range(HEADS):
            att_ref[:, hh * 128 : (hh + 1) * 128] = got_own[hh]

    @pl.when(is_late)
    def _():
        all_own_stat(others).wait_recv()
        all_far(everyone).wait_recv()
        all_far_stat(everyone).wait_recv()
        pad = jnp.zeros((128 - HEADS, 128), jnp.float32)
        stat_a = jnp.concatenate([got_stat_own[hh] for hh in range(HEADS)] + [pad], axis=0)
        stat_b = jnp.concatenate([got_stat_far[hh] for hh in range(HEADS)] + [pad], axis=0)
        lse_a = jnp.transpose(stat_a)[:GROUP]
        lse_b = jnp.transpose(stat_b)[:GROUP]
        share_a = 1.0 / (1.0 + jnp.exp2(lse_b - lse_a))
        share_b = 1.0 / (1.0 + jnp.exp2(lse_a - lse_b))
        for hh in range(HEADS):
            merged = (
                got_own[hh].astype(jnp.float32) * share_a[:, hh : hh + 1]
                + got_far[hh].astype(jnp.float32) * share_b[:, hh : hh + 1]
            )
            att_ref[:, hh * 128 : (hh + 1) * 128] = merged.astype(jnp.bfloat16)

    def col_arrived(j, carry):
        block = lax.rem(w + j, HALF)
        copy(
            column_out.at[block], column_in.at[block], col_send.at[block], col_recv.at[block],
            half_device(block),
        ).wait_recv()
        return carry

    lax.fori_loop(1, HALF, col_arrived, 0)
    heavy = column_in[0]
    for j in range(1, HALF):
        heavy = heavy + column_in[j]
    heavy_ref[...] = heavy

    for slot in range(7):
        k_copy(w, slot, w_core).wait_send()
        v_copy(w, slot, w_core).wait_send()

    all_own(others).wait_send()

    @pl.when(is_late)
    def _():
        all_own_stat(others).wait_send()

    @pl.when(is_early)
    def _():
        all_far(everyone).wait_send()
        all_far_stat(everyone).wait_send()

    def chunk_left(ci, carry):
        peer_copy(stat_own, ci).wait_send()

        @pl.when(is_late)
        def _():
            q_copy(ci).wait_send()

        return carry

    lax.fori_loop(0, CHUNKS, chunk_left, 0)

    def col_left(j, carry):
        col_copy(lax.rem(w + j, HALF)).wait_send()
        return carry

    lax.fori_loop(1, HALF, col_left, 0)


def local(queries, key_states, value_states):
    bf16, f32 = jnp.bfloat16, jnp.float32
    vmem, dma = pltpu.VMEM, pltpu.SemaphoreType.DMA
    whole = pl.BlockSpec(memory_space=pltpu.VMEM)
    quarter = HALF // 2
    return pl.pallas_call(
        kernel,
        out_shape=(
            jax.ShapeDtypeStruct((GROUP, HEADS * DIM), bf16),
            jax.ShapeDtypeStruct((1, ROWS), f32),
        ),
        in_specs=[whole] * 3,
        out_specs=(whole, whole),
        scratch_shapes=[
            vmem((HALF, ROWS, DIM), bf16),
            vmem((HALF, ROWS, DIM), bf16),
            vmem((ROWS, DIM), bf16),
            vmem((HALF, ROWS, ROWS), bf16),
            vmem((HALF, ROWS, 128), f32),
            vmem((HALF, ROWS, 128), f32),
            vmem((HALF, ROWS, DIM), f32),
            vmem((quarter, ROWS, WIDE), bf16),
            vmem((quarter, ROWS, 128), f32),
            vmem((quarter, CHUNK, 128), f32),
            vmem((quarter, CHUNK, DIM), f32),
            vmem((ROWS, 128), f32),
            vmem((HEADS, GROUP, DIM), bf16),
            vmem((HEADS, GROUP, DIM), bf16),
            vmem((CHUNKS, 1, 256), f32),
            vmem((CHUNKS, 1, 256), f32),
            vmem((CHUNKS, 1, 256), f32),
            vmem((HEADS, 1, 128), f32),
            vmem((HEADS, 1, 128), f32),
            vmem((HEADS, GROUP, DIM), bf16),
            vmem((HEADS, GROUP, DIM), bf16),
            vmem((HEADS, 1, 128), f32),
            vmem((HEADS, 1, 128), f32),
            vmem((HALF, 8, ROWS), f32),
            vmem((HALF, 1, ROWS), f32),
            vmem((HALF, 1, ROWS), f32),
            dma((7,)), dma((HALF,)), dma((7,)), dma((HALF,)), dma((CHUNKS,)), dma((CHUNKS,)),
            dma((1,)), dma((1,)), dma((1,)), dma((1,)),
            dma((1,)), dma((1,)), dma((1,)), dma((1,)),
            dma((CHUNKS,)), dma((CHUNKS,)), dma((HALF,)), dma((HALF,)),
            pltpu.SemaphoreType.REGULAR((5,)),
        ],
        compiler_params=pltpu.CompilerParams(
            collective_id=0, has_side_effects=True, vmem_limit_bytes=58 * 1024 * 1024
        ),
    )(queries, key_states, value_states)


def solution(mesh):
    placed = (P("blk", "head"), P("blk", "head"), P("blk", "head"))
    return jax.shard_map(
        local,
        mesh=mesh,
        in_specs=placed,
        out_specs=(P(("blk", "head"), None), P("head", "blk")),
        check_vma=False,
    )
```

```python
import functools
import math

import jax
import jax.numpy as jnp
from jax import lax
from jax.experimental import pallas as pl
from jax.experimental.pallas import tpu as pltpu
from jax.sharding import PartitionSpec as P

MESH = pl.DeviceIdType.MESH
DIM = 128
ROWS = 768
HEADS = 32
HALF = 8
CHUNK = 192
CHUNKS = ROWS // CHUNK
GROUP = ROWS // HEADS
GROUPS = CHUNK // GROUP
TILE = 384
WIDE = 3072
PER = WIDE // ROWS
TILES = HALF // PER
SCALE = math.log2(math.e) / math.sqrt(DIM)
LOW = -1e30


def dot_rows(a, b):
    return lax.dot_general(a, b, (((1,), (1,)), ((), ())), preferred_element_type=jnp.float32)


def dot(a, b):
    return lax.dot_general(a, b, (((1,), (0,)), ((), ())), preferred_element_type=jnp.float32)


def fold_lanes(value, op):
    out = value[:, :128]
    for u in range(1, value.shape[1] // 128):
        out = op(out, value[:, u * 128 : (u + 1) * 128])
    return out


def weigh(logits, values):
    top = jnp.max(fold_lanes(logits, jnp.maximum), axis=1, keepdims=True)
    expo = jnp.exp2((logits - top) * SCALE)
    total = fold_lanes(expo, jnp.add)
    weights = expo.astype(jnp.bfloat16)
    return top, total, weights, dot(weights, values)


def to_lanes(column):
    out = []
    for begin, size in ((0, 128), (128, 64)):
        part = column[begin : begin + size]
        row = lax.broadcasted_iota(jnp.int32, part.shape, 0)
        lane = lax.broadcasted_iota(jnp.int32, part.shape, 1)
        out.append(jnp.sum(jnp.where(row == lane, part, 0.0), axis=0, keepdims=True))
    return out


def to_groups(column):
    parts = column.reshape(GROUPS, GROUP, 128)
    row = lax.broadcasted_iota(jnp.int32, parts.shape, 1)
    lane = lax.broadcasted_iota(jnp.int32, parts.shape, 2)
    return jnp.sum(jnp.where(row == lane, parts, 0.0), axis=1, keepdims=True)


def to_column(row):
    parts = []
    for begin, size in ((0, 128), (128, 64)):
        square = jnp.broadcast_to(row[:, begin : begin + 128], (128, 128))
        parts.append(jnp.transpose(square)[:size])
    return jnp.concatenate(parts, axis=0)


def kernel(
    q_ref, k_ref, v_ref, att_ref, heavy_ref,
    keys, values, q_far, weights_tri, top_tri, total_tri, out_tri,
    weights_far, top_far, total_far, out_far, lse_col,
    send_own, send_far, stat_own, stat_far, stat_peer,
    tag_own, tag_far, got_own, got_far, got_stat_own, got_stat_far,
    column, column_out, column_in,
    k_send, k_recv, v_send, v_recv, q_send, q_recv,
    own_send, own_recv, own_stat_send, own_stat_recv,
    far_send, far_recv, far_stat_send, far_stat_recv,
    peer_send, peer_recv, col_send, col_recv, ready, local_sem, q_own,
):
    h = lax.axis_index("head")
    b = lax.axis_index("blk")
    later = b // HALF
    w = lax.rem(b, HALF)
    y, core = w // 2, lax.rem(w, 2)
    x, z = h // 8, lax.rem(h, 8)
    base = later * HALF
    is_early, is_late = later == 0, later == 1

    def place(dy, flip):
        yy = lax.rem(y + dy, 4)
        return yy * 2 + (lax.rem(core + flip, 2))

    def half_device(block):
        return (h, base + block)

    partner = (h, w + (1 - later) * HALF)
    w_right, w_left, w_core = place(1, 0), place(3, 0), place(0, 1)

    def copy(src, dst, send_sem, recv_sem, device):
        return pltpu.make_async_remote_copy(
            src_ref=src, dst_ref=dst, send_sem=send_sem, recv_sem=recv_sem,
            device_id=device, device_id_type=MESH,
        )

    barrier = pltpu.get_barrier_semaphore()

    def greet(device):
        pl.semaphore_signal(barrier, inc=1, device_id=device, device_id_type=MESH)

    def along_z(step):
        return ((z >= step, (h - step, b)), (z + step < 8, (h + step, b)))

    def along_x():
        return [(lax.rem(h + 8 * d, HEADS), b) for d in (1, 2, 3)]

    def count_z(step):
        return (z >= step).astype(jnp.int32) + (z + step < 8).astype(jnp.int32)

    for exists, device in along_z(1):
        pl.when(exists)(functools.partial(greet, device))
    for device in along_x():
        greet(device)
    for block in (w_right, w_left, w_core):
        greet(half_device(block))
    pl.when(is_early)(functools.partial(greet, partner))

    def tell(index, device):
        pl.semaphore_signal(ready.at[index], inc=1, device_id=device, device_id_type=MESH)

    def tell_z(index, step):
        for exists, device in along_z(step):
            pl.when(exists)(functools.partial(tell, index, device))

    def hear(index, count):
        pl.semaphore_wait(ready.at[index], count)

    inside = [
        pltpu.make_async_copy(src, dst, local_sem.at[n])
        for n, (src, dst) in enumerate(((q_ref, q_own), (k_ref, keys.at[w]), (v_ref, values.at[w])))
    ]
    for one in inside:
        one.start()

    def triangle(block, masked, tiles):
        for t in tiles:
            rows = pl.ds(t * TILE, TILE)
            logits = dot_rows(q_own[rows, :], keys[block])
            if masked:
                row = lax.broadcasted_iota(jnp.int32, logits.shape, 0) + t * TILE
                col = lax.broadcasted_iota(jnp.int32, logits.shape, 1)
                logits = jnp.where(col <= row, logits, LOW)
            top, total, weights, out = weigh(logits, values[block])
            weights_tri[block, rows, :] = weights
            top_tri[block, rows, :] = jnp.broadcast_to(top, (TILE, 128))
            total_tri[block, rows, :] = total
            out_tri[block, rows, :] = out

    pl.semaphore_wait(barrier, 6 + count_z(1) + later)

    def q_copy(ci):
        rows = pl.ds(pl.multiple_of(ci * CHUNK, CHUNK), CHUNK)
        return copy(q_ref.at[rows], q_far.at[rows], q_send.at[ci], q_recv.at[ci], partner)

    def send_queries(i):
        pl.when(is_late)(lambda: q_copy(lax.rem(x + i, CHUNKS)).start())

    send_queries(0)

    def k_copy(block, slot, to):
        return copy(keys.at[block], keys.at[block], k_send.at[slot], k_recv.at[block], half_device(to))

    def v_copy(block, slot, to):
        return copy(values.at[block], values.at[block], v_send.at[slot], v_recv.at[block], half_device(to))

    def own_copy_out(src, dst, send_sem, recv_sem, slot, to):
        return copy(src, dst.at[w], send_sem.at[slot], recv_sem.at[w], half_device(to))

    def k_out(slot, to):
        own_copy_out(k_ref, keys, k_send, k_recv, slot, to).start()

    def v_out(slot, to):
        own_copy_out(v_ref, values, v_send, v_recv, slot, to).start()

    k_out(0, w_right)
    v_out(1, w_left)
    k_out(2, w_core)
    v_out(2, w_core)
    v_out(0, w_right)
    k_out(1, w_left)

    tell_z(0, 1)
    for one in inside:
        one.wait()
    triangle(w, True, (0,))
    hear(0, count_z(1))
    tell_z(1, 2)
    triangle(w, True, (1,))
    hear(1, count_z(2))
    tell_z(2, 4)
    send_queries(1)
    column[...] = jnp.zeros_like(column)

    def k_wait(block):
        k_copy(block, 0, w_core).wait_recv()

    def v_wait(block):
        v_copy(block, 0, w_core).wait_recv()

    def own_copy(hg):
        return copy(send_own.at[hg], got_own.at[h], own_send.at[0], own_recv.at[0], (hg, b))

    def own_stat_copy(hg):
        return copy(
            tag_own.at[hg], got_stat_own.at[h],
            own_stat_send.at[0], own_stat_recv.at[0], (hg, b),
        )

    def far_copy(hg):
        return copy(send_far.at[hg], got_far.at[h], far_send.at[0], far_recv.at[0], (hg, w + HALF))

    def far_stat_copy(hg):
        return copy(
            tag_far.at[hg], got_stat_far.at[h],
            far_stat_send.at[0], far_stat_recv.at[0], (hg, w + HALF),
        )

    def peer_copy(stat, ci):
        return copy(stat.at[ci], stat_peer.at[ci], peer_send.at[ci], peer_recv.at[ci], partner)

    def settle(count, rows, tops, totals, outs):
        top = lax.fori_loop(
            1, count, lambda j, top: jnp.maximum(top, tops[j, rows, :]), tops[0, rows, :]
        )

        def add(j, carry):
            total, out = carry
            factor = jnp.exp2((tops[j, rows, :] - top) * SCALE)
            return (total + factor * totals[j, rows, :], out + factor * outs[j, rows, :])

        zero = jnp.zeros((CHUNK, 128), jnp.float32)
        total, out = lax.fori_loop(0, count, add, (zero, zero))
        total = jnp.sum(total, axis=1, keepdims=True)
        return out * (1.0 / total), top * SCALE + jnp.log2(total)

    def settle_triangle():
        def chunk(ci, carry):
            rows = pl.ds(pl.multiple_of(ci * CHUNK, CHUNK), CHUNK)
            out, lse = settle(w + 1, rows, top_tri, total_tri, out_tri)
            send_own[pl.ds(ci * GROUPS, GROUPS)] = out.reshape(GROUPS, GROUP, DIM).astype(jnp.bfloat16)
            lse_col[rows, :] = lse
            tag_own[pl.ds(ci * GROUPS, GROUPS)] = to_groups(lse)
            low, high = to_lanes(lse)
            stat_own[ci, :, :128] = low
            stat_own[ci, :, 128:] = high
            return carry

        lax.fori_loop(0, CHUNKS, chunk, 0)

        @pl.when(is_late)
        def _():
            for ci in range(CHUNKS):
                peer_copy(stat_own, ci).start()

        got_own[h] = send_own[h]

        def start(j, carry):
            hg = lax.rem(h + j, HEADS)
            own_copy(hg).start()

            @pl.when(is_late)
            def _():
                own_stat_copy(hg).start()

            return carry

        lax.fori_loop(1, HEADS, start, 0)

        @pl.when(is_late)
        def _():
            got_stat_own[h] = tag_own[h]

    def rectangle(ci, first):
        q_copy(ci).wait_recv()
        rows = pl.ds(pl.multiple_of(ci * CHUNK, CHUNK), CHUNK)
        local = pl.ds(0, CHUNK)

        def step(d, carry):
            blocks = pl.ds(d * PER, PER)
            key_tile = keys[blocks].reshape(WIDE, DIM)
            value_tile = values[blocks].reshape(WIDE, DIM)
            logits = dot_rows(q_far[rows, :], key_tile)
            top, total, weights, out = weigh(logits, value_tile)
            weights_far[d, rows, :] = weights
            top_far[d, rows, :] = jnp.broadcast_to(top, (CHUNK, 128))
            total_far[d, local, :] = total
            out_far[d, local, :] = out
            return carry

        for d in range(TILES):
            step(d, 0)
        top = top_far[0, rows, :]
        for d in range(1, TILES):
            top = jnp.maximum(top, top_far[d, rows, :])
        total = jnp.zeros((CHUNK, 128), jnp.float32)
        out = jnp.zeros((CHUNK, 128), jnp.float32)
        for d in range(TILES):
            factor = jnp.exp2((top_far[d, rows, :] - top) * SCALE)
            total = total + factor * total_far[d]
            out = out + factor * out_far[d]
        total = jnp.sum(total, axis=1, keepdims=True)
        out = out * (1.0 / total)
        send_far[pl.ds(ci * GROUPS, GROUPS)] = out.reshape(GROUPS, GROUP, DIM).astype(jnp.bfloat16)
        lse = top * SCALE + jnp.log2(total)
        tag_far[pl.ds(ci * GROUPS, GROUPS)] = to_groups(lse)
        low, high = to_lanes(lse)
        stat_far[ci, :, :128] = low
        stat_far[ci, :, 128:] = high

        pl.when(first)(functools.partial(hear, 4, 1))

        def start(g, carry):
            hg = ci * GROUPS + lax.rem(z + g, GROUPS)
            far_copy(hg).start()
            far_stat_copy(hg).start()
            return carry

        lax.fori_loop(0, GROUPS, start, 0)
        peer_copy(stat_far, ci).start()

    def step(i, carry):
        @pl.when(i == 1)
        def _():
            k_wait(w_core)
            v_wait(w_core)

        @pl.when(i == 2)
        def _():
            hear(2, count_z(4))
            for device in along_x():
                tell(3, device)
            hear(3, 3)
            pl.when(is_late)(functools.partial(tell, 4, partner))
            send_queries(2)
            k_wait(w_left)
            k_copy(w_left, 3, w_right).start()
            k_copy(w_left, 4, w_core).start()
            v_wait(w_right)
            v_copy(w_right, 3, w_left).start()
            v_copy(w_right, 5, w_core).start()
            v_wait(w_left)
            v_copy(w_left, 4, w_core).start()
            k_wait(w_right)
            k_copy(w_right, 5, w_core).start()

        @pl.when(i == 4)
        def _():
            send_queries(3)
            for dy in (3, 1):
                k_wait(place(dy, 1))
                v_wait(place(dy, 1))

        @pl.when(i == 6)
        def _():
            far_block = place(2, 0)
            k_wait(far_block)
            k_copy(far_block, 6, w_core).start()
            v_wait(far_block)
            v_copy(far_block, 6, w_core).start()
            k_wait(place(2, 1))
            v_wait(place(2, 1))

        @pl.when(jnp.logical_and(is_early, jnp.logical_and(i >= 6, i != 8)))
        def _():
            rectangle(lax.rem(x + jnp.where(i < 8, i - 6, i - 7), CHUNKS), i == 6)

        def unit(u, carry):
            dy = jnp.where(u == 1, 0, jnp.where(u >= 6, 2, jnp.where(lax.rem(u, 2) == 0, 3, 1)))
            flip = jnp.where(jnp.logical_or(u == 1, jnp.logical_or(u == 4, jnp.logical_or(u == 5, u == 7))), 1, 0)
            block = place(dy, flip)

            @pl.when(block < w)
            def _():
                triangle(block, False, range(ROWS // TILE))

            return carry

        first = jnp.where(i <= 5, i, 6)
        last = jnp.where(i <= 5, i + 1, jnp.where(i == 8, 8, 6))
        lax.fori_loop(first, last, unit, 0)

        @pl.when(i == jnp.where(y <= 1, 5, 8))
        def _():
            settle_triangle()

        return carry

    lax.fori_loop(1, 11, step, 0)

    def add_columns(count, rows, tops, weights, lse, width):
        per = width // ROWS

        def tile(j, carry):
            factor = jnp.exp2(tops[j, rows, :] * SCALE - lse)
            for u in range(width // 128):
                part = weights[j, rows, u * 128 : (u + 1) * 128].astype(jnp.float32) * factor
                part = jnp.sum(part.reshape(CHUNK // 8, 8, 128), axis=0)
                lanes = slice(u % 6 * 128, u % 6 * 128 + 128)
                column[j * per + u // 6, :, lanes] += part
            return carry

        lax.fori_loop(0, count, tile, 0)

    def both(one, two):
        top = jnp.maximum(one, two)
        return top + jnp.log2(jnp.exp2(one - top) + jnp.exp2(two - top))

    def piece(i):
        ci = lax.rem(x + i, CHUNKS)
        return ci, pl.ds(pl.multiple_of(ci * CHUNK, CHUNK), CHUNK)

    @pl.when(is_early)
    def _():
        def near(i, carry):
            ci, rows = piece(i)
            add_columns(w + 1, rows, top_tri, weights_tri, lse_col[rows, :], ROWS)
            return carry

        lax.fori_loop(0, CHUNKS, near, 0)

        def distant(i, carry):
            ci, rows = piece(i)
            peer_copy(stat_own, ci).wait_recv()
            lse = to_column(both(stat_far[ci], stat_peer[ci]))
            add_columns(TILES, rows, top_far, weights_far, lse, WIDE)
            return carry

        lax.fori_loop(0, CHUNKS, distant, 0)

    @pl.when(is_late)
    def _():
        def near(i, carry):
            ci, rows = piece(i)
            peer_copy(stat_own, ci).wait_recv()
            lse = to_column(both(stat_own[ci], stat_peer[ci]))
            add_columns(w + 1, rows, top_tri, weights_tri, lse, ROWS)
            return carry

        lax.fori_loop(0, CHUNKS, near, 0)

    for j in range(HALF):
        column_out[j] = jnp.sum(column[j], axis=0, keepdims=True)

    def col_copy(block):
        return copy(
            column_out.at[block], column_in.at[w], col_send.at[block], col_recv.at[w], half_device(block)
        )

    def col_start(j, carry):
        col_copy(lax.rem(w + j, HALF)).start()
        return carry

    lax.fori_loop(1, HALF, col_start, 0)
    column_in[w] = column_out[w]

    others, everyone = pl.ds(0, HEADS - 1), pl.ds(0, HEADS)

    def all_own(which):
        return copy(
            send_own.at[which], got_own.at[which], own_send.at[0], own_recv.at[0], half_device(w_core)
        )

    def all_own_stat(which):
        return copy(
            tag_own.at[which], got_stat_own.at[which],
            own_stat_send.at[0], own_stat_recv.at[0], half_device(w_core),
        )

    def all_far(which):
        return copy(
            send_far.at[which], got_far.at[which], far_send.at[0], far_recv.at[0], partner
        )

    def all_far_stat(which):
        return copy(
            tag_far.at[which], got_stat_far.at[which],
            far_stat_send.at[0], far_stat_recv.at[0], partner,
        )

    all_own(others).wait_recv()

    @pl.when(is_early)
    def _():
        for hh in range(HEADS):
            att_ref[:, hh * 128 : (hh + 1) * 128] = got_own[hh]

    @pl.when(is_late)
    def _():
        all_own_stat(others).wait_recv()
        all_far(everyone).wait_recv()
        all_far_stat(everyone).wait_recv()
        pad = jnp.zeros((128 - HEADS, 128), jnp.float32)
        stat_a = jnp.concatenate([got_stat_own[hh] for hh in range(HEADS)] + [pad], axis=0)
        stat_b = jnp.concatenate([got_stat_far[hh] for hh in range(HEADS)] + [pad], axis=0)
        lse_a = jnp.transpose(stat_a)[:GROUP]
        lse_b = jnp.transpose(stat_b)[:GROUP]
        share_a = 1.0 / (1.0 + jnp.exp2(lse_b - lse_a))
        share_b = 1.0 / (1.0 + jnp.exp2(lse_a - lse_b))
        for hh in range(HEADS):
            merged = (
                got_own[hh].astype(jnp.float32) * share_a[:, hh : hh + 1]
                + got_far[hh].astype(jnp.float32) * share_b[:, hh : hh + 1]
            )
            att_ref[:, hh * 128 : (hh + 1) * 128] = merged.astype(jnp.bfloat16)

    def col_arrived(j, carry):
        block = lax.rem(w + j, HALF)
        copy(
            column_out.at[block], column_in.at[block], col_send.at[block], col_recv.at[block],
            half_device(block),
        ).wait_recv()
        return carry

    lax.fori_loop(1, HALF, col_arrived, 0)
    heavy = column_in[0]
    for j in range(1, HALF):
        heavy = heavy + column_in[j]
    heavy_ref[...] = heavy

    for slot in range(7):
        k_copy(w, slot, w_core).wait_send()
        v_copy(w, slot, w_core).wait_send()

    all_own(others).wait_send()

    @pl.when(is_late)
    def _():
        all_own_stat(others).wait_send()

    @pl.when(is_early)
    def _():
        all_far(everyone).wait_send()
        all_far_stat(everyone).wait_send()

    def chunk_left(ci, carry):
        peer_copy(stat_own, ci).wait_send()

        @pl.when(is_late)
        def _():
            q_copy(ci).wait_send()

        return carry

    lax.fori_loop(0, CHUNKS, chunk_left, 0)

    def col_left(j, carry):
        col_copy(lax.rem(w + j, HALF)).wait_send()
        return carry

    lax.fori_loop(1, HALF, col_left, 0)


def local(queries, key_states, value_states):
    bf16, f32 = jnp.bfloat16, jnp.float32
    vmem, dma = pltpu.VMEM, pltpu.SemaphoreType.DMA
    whole = pl.BlockSpec(memory_space=pltpu.VMEM)
    return pl.pallas_call(
        kernel,
        out_shape=(
            jax.ShapeDtypeStruct((GROUP, HEADS * DIM), bf16),
            jax.ShapeDtypeStruct((1, ROWS), f32),
        ),
        in_specs=[pl.BlockSpec(memory_space=pl.ANY)] * 3,
        out_specs=(whole, whole),
        scratch_shapes=[
            vmem((HALF, ROWS, DIM), bf16),
            vmem((HALF, ROWS, DIM), bf16),
            vmem((ROWS, DIM), bf16),
            vmem((HALF, ROWS, ROWS), bf16),
            vmem((HALF, ROWS, 128), f32),
            vmem((HALF, ROWS, 128), f32),
            vmem((HALF, ROWS, DIM), f32),
            vmem((TILES, ROWS, WIDE), bf16),
            vmem((TILES, ROWS, 128), f32),
            vmem((TILES, CHUNK, 128), f32),
            vmem((TILES, CHUNK, DIM), f32),
            vmem((ROWS, 128), f32),
            vmem((HEADS, GROUP, DIM), bf16),
            vmem((HEADS, GROUP, DIM), bf16),
            vmem((CHUNKS, 1, 256), f32),
            vmem((CHUNKS, 1, 256), f32),
            vmem((CHUNKS, 1, 256), f32),
            vmem((HEADS, 1, 128), f32),
            vmem((HEADS, 1, 128), f32),
            vmem((HEADS, GROUP, DIM), bf16),
            vmem((HEADS, GROUP, DIM), bf16),
            vmem((HEADS, 1, 128), f32),
            vmem((HEADS, 1, 128), f32),
            vmem((HALF, 8, ROWS), f32),
            vmem((HALF, 1, ROWS), f32),
            vmem((HALF, 1, ROWS), f32),
            dma((7,)), dma((HALF,)), dma((7,)), dma((HALF,)), dma((CHUNKS,)), dma((CHUNKS,)),
            dma((1,)), dma((1,)), dma((1,)), dma((1,)),
            dma((1,)), dma((1,)), dma((1,)), dma((1,)),
            dma((CHUNKS,)), dma((CHUNKS,)), dma((HALF,)), dma((HALF,)),
            pltpu.SemaphoreType.REGULAR((5,)),
            dma((3,)),
            vmem((ROWS, DIM), bf16),
        ],
        compiler_params=pltpu.CompilerParams(
            collective_id=0, has_side_effects=True, vmem_limit_bytes=58 * 1024 * 1024
        ),
    )(queries, key_states, value_states)


def solution(mesh):
    placed = (P("blk", "head"), P("blk", "head"), P("blk", "head"))
    return jax.shard_map(
        local,
        mesh=mesh,
        in_specs=placed,
        out_specs=(P(("blk", "head"), None), P("head", "blk")),
        check_vma=False,
    )
```

```python
import functools
import math

import jax
import jax.numpy as jnp
from jax import lax
from jax.experimental import pallas as pl
from jax.experimental.pallas import tpu as pltpu
from jax.sharding import PartitionSpec as P

MESH = pl.DeviceIdType.MESH
DIM = 128
ROWS = 768
HEADS = 32
HALF = 8
CHUNK = 192
CHUNKS = ROWS // CHUNK
GROUP = ROWS // HEADS
GROUPS = CHUNK // GROUP
TILE = 384
WIDE = 3072
PER = WIDE // ROWS
TILES = HALF // PER
SCALE = math.log2(math.e) / math.sqrt(DIM)
LOW = -1e30


def dot_rows(a, b):
    return lax.dot_general(a, b, (((1,), (1,)), ((), ())), preferred_element_type=jnp.float32)


def dot(a, b):
    return lax.dot_general(a, b, (((1,), (0,)), ((), ())), preferred_element_type=jnp.float32)


def fold_lanes(value, op):
    out = value[:, :128]
    for u in range(1, value.shape[1] // 128):
        out = op(out, value[:, u * 128 : (u + 1) * 128])
    return out


def weigh(logits, values):
    top = jnp.max(fold_lanes(logits, jnp.maximum), axis=1, keepdims=True)
    expo = jnp.exp2((logits - top) * SCALE)
    total = fold_lanes(expo, jnp.add)
    weights = expo.astype(jnp.bfloat16)
    return top, total, weights, dot(weights, values)


def to_lanes(column):
    out = []
    for begin, size in ((0, 128), (128, 64)):
        part = column[begin : begin + size]
        row = lax.broadcasted_iota(jnp.int32, part.shape, 0)
        lane = lax.broadcasted_iota(jnp.int32, part.shape, 1)
        out.append(jnp.sum(jnp.where(row == lane, part, 0.0), axis=0, keepdims=True))
    return out


def to_groups(column):
    parts = column.reshape(GROUPS, GROUP, 128)
    row = lax.broadcasted_iota(jnp.int32, parts.shape, 1)
    lane = lax.broadcasted_iota(jnp.int32, parts.shape, 2)
    return jnp.sum(jnp.where(row == lane, parts, 0.0), axis=1, keepdims=True)


def to_column(row):
    parts = []
    for begin, size in ((0, 128), (128, 64)):
        square = jnp.broadcast_to(row[:, begin : begin + 128], (128, 128))
        parts.append(jnp.transpose(square)[:size])
    return jnp.concatenate(parts, axis=0)


def kernel(
    q_ref, k_ref, v_ref, att_ref, heavy_ref,
    keys, values, q_far, weights_tri, top_tri, total_tri, out_tri,
    weights_far, top_far, total_far, out_far, lse_col,
    send_own, send_far, stat_own, stat_far, stat_peer,
    tag_own, tag_far, got_own, got_far, got_stat_own, got_stat_far,
    column, column_out, column_in,
    k_send, k_recv, v_send, v_recv, q_send, q_recv,
    own_send, own_recv, own_stat_send, own_stat_recv,
    far_send, far_recv, far_stat_send, far_stat_recv,
    peer_send, peer_recv, col_send, col_recv, ready, local_sem, q_own,
):
    h = lax.axis_index("head")
    b = lax.axis_index("blk")
    later = b // HALF
    w = lax.rem(b, HALF)
    y, core = w // 2, lax.rem(w, 2)
    x, z = h // 8, lax.rem(h, 8)
    base = later * HALF
    is_early, is_late = later == 0, later == 1

    def place(dy, flip):
        yy = lax.rem(y + dy, 4)
        return yy * 2 + (lax.rem(core + flip, 2))

    def half_device(block):
        return (h, base + block)

    partner = (h, w + (1 - later) * HALF)
    w_right, w_left, w_core = place(1, 0), place(3, 0), place(0, 1)

    def copy(src, dst, send_sem, recv_sem, device):
        return pltpu.make_async_remote_copy(
            src_ref=src, dst_ref=dst, send_sem=send_sem, recv_sem=recv_sem,
            device_id=device, device_id_type=MESH,
        )

    barrier = pltpu.get_barrier_semaphore()

    def greet(device):
        pl.semaphore_signal(barrier, inc=1, device_id=device, device_id_type=MESH)

    def along_z(step):
        return ((z >= step, (h - step, b)), (z + step < 8, (h + step, b)))

    def along_x():
        return [(lax.rem(h + 8 * d, HEADS), b) for d in (1, 2, 3)]

    def count_z(step):
        return (z >= step).astype(jnp.int32) + (z + step < 8).astype(jnp.int32)

    for exists, device in along_z(1):
        pl.when(exists)(functools.partial(greet, device))
    for device in along_x():
        greet(device)
    for block in (w_right, w_left, w_core):
        greet(half_device(block))
    pl.when(is_early)(functools.partial(greet, partner))

    def tell(index, device):
        pl.semaphore_signal(ready.at[index], inc=1, device_id=device, device_id_type=MESH)

    def tell_z(index, step):
        for exists, device in along_z(step):
            pl.when(exists)(functools.partial(tell, index, device))

    def hear(index, count):
        pl.semaphore_wait(ready.at[index], count)

    inside = [
        pltpu.make_async_copy(src, dst, local_sem.at[n])
        for n, (src, dst) in enumerate(((q_ref, q_own), (k_ref, keys.at[w]), (v_ref, values.at[w])))
    ]
    for one in inside:
        one.start()

    def triangle(block, masked, tiles):
        for t in tiles:
            rows = pl.ds(t * TILE, TILE)
            logits = dot_rows(q_own[rows, :], keys[block])
            if masked:
                row = lax.broadcasted_iota(jnp.int32, logits.shape, 0) + t * TILE
                col = lax.broadcasted_iota(jnp.int32, logits.shape, 1)
                logits = jnp.where(col <= row, logits, LOW)
            top, total, weights, out = weigh(logits, values[block])
            weights_tri[block, rows, :] = weights
            top_tri[block, rows, :] = jnp.broadcast_to(top, (TILE, 128))
            total_tri[block, rows, :] = total
            out_tri[block, rows, :] = out

    pl.semaphore_wait(barrier, 6 + count_z(1) + later)

    def q_copy(ci):
        rows = pl.ds(pl.multiple_of(ci * CHUNK, CHUNK), CHUNK)
        return copy(q_ref.at[rows], q_far.at[rows], q_send.at[ci], q_recv.at[ci], partner)

    def send_queries(i):
        pl.when(is_late)(lambda: q_copy(lax.rem(x + i, CHUNKS)).start())

    send_queries(0)

    def k_copy(block, slot, to):
        return copy(keys.at[block], keys.at[block], k_send.at[slot], k_recv.at[block], half_device(to))

    def v_copy(block, slot, to):
        return copy(values.at[block], values.at[block], v_send.at[slot], v_recv.at[block], half_device(to))

    def own_copy_out(src, dst, send_sem, recv_sem, slot, to):
        return copy(src, dst.at[w], send_sem.at[slot], recv_sem.at[w], half_device(to))

    def k_out(slot, to):
        own_copy_out(k_ref, keys, k_send, k_recv, slot, to).start()

    def v_out(slot, to):
        own_copy_out(v_ref, values, v_send, v_recv, slot, to).start()

    k_out(0, w_right)
    v_out(1, w_left)
    k_out(2, w_core)
    v_out(2, w_core)
    v_out(0, w_right)
    k_out(1, w_left)

    tell_z(0, 1)
    for one in inside:
        one.wait()
    triangle(w, True, (0,))
    hear(0, count_z(1))
    tell_z(1, 2)
    triangle(w, True, (1,))
    hear(1, count_z(2))
    tell_z(2, 4)
    send_queries(1)
    column[...] = jnp.zeros_like(column)

    def k_wait(block):
        k_copy(block, 0, w_core).wait_recv()

    def v_wait(block):
        v_copy(block, 0, w_core).wait_recv()

    k_wait(w_left)
    k_copy(w_left, 3, w_right).start()
    v_wait(w_right)
    v_copy(w_right, 3, w_left).start()

    def own_copy(hg):
        return copy(send_own.at[hg], got_own.at[h], own_send.at[0], own_recv.at[0], (hg, b))

    def own_stat_copy(hg):
        return copy(
            tag_own.at[hg], got_stat_own.at[h],
            own_stat_send.at[0], own_stat_recv.at[0], (hg, b),
        )

    def far_copy(hg):
        return copy(send_far.at[hg], got_far.at[h], far_send.at[0], far_recv.at[0], (hg, w + HALF))

    def far_stat_copy(hg):
        return copy(
            tag_far.at[hg], got_stat_far.at[h],
            far_stat_send.at[0], far_stat_recv.at[0], (hg, w + HALF),
        )

    def peer_copy(stat, ci):
        return copy(stat.at[ci], stat_peer.at[ci], peer_send.at[ci], peer_recv.at[ci], partner)

    def settle(count, rows, tops, totals, outs):
        top = lax.fori_loop(
            1, count, lambda j, top: jnp.maximum(top, tops[j, rows, :]), tops[0, rows, :]
        )

        def add(j, carry):
            total, out = carry
            factor = jnp.exp2((tops[j, rows, :] - top) * SCALE)
            return (total + factor * totals[j, rows, :], out + factor * outs[j, rows, :])

        zero = jnp.zeros((CHUNK, 128), jnp.float32)
        total, out = lax.fori_loop(0, count, add, (zero, zero))
        total = jnp.sum(total, axis=1, keepdims=True)
        return out * (1.0 / total), top * SCALE + jnp.log2(total)

    def settle_triangle():
        def chunk(ci, carry):
            rows = pl.ds(pl.multiple_of(ci * CHUNK, CHUNK), CHUNK)
            out, lse = settle(w + 1, rows, top_tri, total_tri, out_tri)
            send_own[pl.ds(ci * GROUPS, GROUPS)] = out.reshape(GROUPS, GROUP, DIM).astype(jnp.bfloat16)
            lse_col[rows, :] = lse
            tag_own[pl.ds(ci * GROUPS, GROUPS)] = to_groups(lse)
            low, high = to_lanes(lse)
            stat_own[ci, :, :128] = low
            stat_own[ci, :, 128:] = high
            return carry

        lax.fori_loop(0, CHUNKS, chunk, 0)

        @pl.when(is_late)
        def _():
            for ci in range(CHUNKS):
                peer_copy(stat_own, ci).start()

        got_own[h] = send_own[h]

        def start(j, carry):
            hg = lax.rem(h + j, HEADS)
            own_copy(hg).start()

            @pl.when(is_late)
            def _():
                own_stat_copy(hg).start()

            return carry

        lax.fori_loop(1, HEADS, start, 0)

        @pl.when(is_late)
        def _():
            got_stat_own[h] = tag_own[h]

    def rectangle(ci, first):
        q_copy(ci).wait_recv()
        rows = pl.ds(pl.multiple_of(ci * CHUNK, CHUNK), CHUNK)
        local = pl.ds(0, CHUNK)

        def step(d, carry):
            blocks = pl.ds(d * PER, PER)
            key_tile = keys[blocks].reshape(WIDE, DIM)
            value_tile = values[blocks].reshape(WIDE, DIM)
            logits = dot_rows(q_far[rows, :], key_tile)
            top, total, weights, out = weigh(logits, value_tile)
            weights_far[d, rows, :] = weights
            top_far[d, rows, :] = jnp.broadcast_to(top, (CHUNK, 128))
            total_far[d, local, :] = total
            out_far[d, local, :] = out
            return carry

        for d in range(TILES):
            step(d, 0)
        top = top_far[0, rows, :]
        for d in range(1, TILES):
            top = jnp.maximum(top, top_far[d, rows, :])
        total = jnp.zeros((CHUNK, 128), jnp.float32)
        out = jnp.zeros((CHUNK, 128), jnp.float32)
        for d in range(TILES):
            factor = jnp.exp2((top_far[d, rows, :] - top) * SCALE)
            total = total + factor * total_far[d]
            out = out + factor * out_far[d]
        total = jnp.sum(total, axis=1, keepdims=True)
        out = out * (1.0 / total)
        send_far[pl.ds(ci * GROUPS, GROUPS)] = out.reshape(GROUPS, GROUP, DIM).astype(jnp.bfloat16)
        lse = top * SCALE + jnp.log2(total)
        tag_far[pl.ds(ci * GROUPS, GROUPS)] = to_groups(lse)
        low, high = to_lanes(lse)
        stat_far[ci, :, :128] = low
        stat_far[ci, :, 128:] = high

        pl.when(first)(functools.partial(hear, 3, 1))

        def start(g, carry):
            hg = ci * GROUPS + lax.rem(z + g, GROUPS)
            far_copy(hg).start()
            far_stat_copy(hg).start()
            return carry

        lax.fori_loop(0, GROUPS, start, 0)
        peer_copy(stat_far, ci).start()

    def step(i, carry):
        @pl.when(i == 1)
        def _():
            hear(2, count_z(4))
            pl.when(is_late)(functools.partial(tell, 3, partner))
            k_wait(w_core)
            v_wait(w_core)

        @pl.when(i == 2)
        def _():
            k_copy(w_left, 4, w_core).start()
            v_copy(w_right, 5, w_core).start()
            send_queries(2)
            v_wait(w_left)
            v_copy(w_left, 4, w_core).start()
            k_wait(w_right)
            k_copy(w_right, 5, w_core).start()

        @pl.when(i == 4)
        def _():
            send_queries(3)
            for dy in (3, 1):
                k_wait(place(dy, 1))
                v_wait(place(dy, 1))

        @pl.when(i == 6)
        def _():
            far_block = place(2, 0)
            k_wait(far_block)
            k_copy(far_block, 6, w_core).start()
            v_wait(far_block)
            v_copy(far_block, 6, w_core).start()
            k_wait(place(2, 1))
            v_wait(place(2, 1))

        @pl.when(jnp.logical_and(is_early, jnp.logical_and(i >= 6, i != 9)))
        def _():
            rectangle(lax.rem(x + jnp.where(i < 9, i - 6, i - 7), CHUNKS), i == 6)

        def unit(u, carry):
            dy = jnp.where(u == 1, 0, jnp.where(u >= 6, 2, jnp.where(lax.rem(u, 2) == 0, 3, 1)))
            flip = jnp.where(jnp.logical_or(u == 1, jnp.logical_or(u == 4, jnp.logical_or(u == 5, u == 7))), 1, 0)
            block = place(dy, flip)

            @pl.when(block < w)
            def _():
                triangle(block, False, range(ROWS // TILE))

            return carry

        first = jnp.where(i <= 5, i, 6)
        last = jnp.where(i <= 5, i + 1, jnp.where(i == 9, 8, 6))
        lax.fori_loop(first, last, unit, 0)

        @pl.when(i == jnp.where(y <= 1, 5, 9))
        def _():
            settle_triangle()

        return carry

    lax.fori_loop(1, 11, step, 0)

    def add_columns(count, rows, tops, weights, lse, width):
        per = width // ROWS

        def tile(j, carry):
            factor = jnp.exp2(tops[j, rows, :] * SCALE - lse)
            for u in range(width // 128):
                part = weights[j, rows, u * 128 : (u + 1) * 128].astype(jnp.float32) * factor
                part = jnp.sum(part.reshape(CHUNK // 8, 8, 128), axis=0)
                lanes = slice(u % 6 * 128, u % 6 * 128 + 128)
                column[j * per + u // 6, :, lanes] += part
            return carry

        lax.fori_loop(0, count, tile, 0)

    def both(one, two):
        top = jnp.maximum(one, two)
        return top + jnp.log2(jnp.exp2(one - top) + jnp.exp2(two - top))

    def piece(i):
        ci = lax.rem(x + i, CHUNKS)
        return ci, pl.ds(pl.multiple_of(ci * CHUNK, CHUNK), CHUNK)

    @pl.when(is_early)
    def _():
        def near(i, carry):
            ci, rows = piece(i)
            add_columns(w + 1, rows, top_tri, weights_tri, lse_col[rows, :], ROWS)
            return carry

        lax.fori_loop(0, CHUNKS, near, 0)

        def distant(i, carry):
            ci, rows = piece(i)
            peer_copy(stat_own, ci).wait_recv()
            lse = to_column(both(stat_far[ci], stat_peer[ci]))
            add_columns(TILES, rows, top_far, weights_far, lse, WIDE)
            return carry

        lax.fori_loop(0, CHUNKS, distant, 0)

    @pl.when(is_late)
    def _():
        def near(i, carry):
            ci, rows = piece(i)
            peer_copy(stat_own, ci).wait_recv()
            lse = to_column(both(stat_own[ci], stat_peer[ci]))
            add_columns(w + 1, rows, top_tri, weights_tri, lse, ROWS)
            return carry

        lax.fori_loop(0, CHUNKS, near, 0)

    for j in range(HALF):
        column_out[j] = jnp.sum(column[j], axis=0, keepdims=True)

    def col_copy(block):
        return copy(
            column_out.at[block], column_in.at[w], col_send.at[block], col_recv.at[w], half_device(block)
        )

    def col_start(j, carry):
        col_copy(lax.rem(w + j, HALF)).start()
        return carry

    lax.fori_loop(1, HALF, col_start, 0)
    column_in[w] = column_out[w]

    others, everyone = pl.ds(0, HEADS - 1), pl.ds(0, HEADS)

    def all_own(which):
        return copy(
            send_own.at[which], got_own.at[which], own_send.at[0], own_recv.at[0], half_device(w_core)
        )

    def all_own_stat(which):
        return copy(
            tag_own.at[which], got_stat_own.at[which],
            own_stat_send.at[0], own_stat_recv.at[0], half_device(w_core),
        )

    def all_far(which):
        return copy(
            send_far.at[which], got_far.at[which], far_send.at[0], far_recv.at[0], partner
        )

    def all_far_stat(which):
        return copy(
            tag_far.at[which], got_stat_far.at[which],
            far_stat_send.at[0], far_stat_recv.at[0], partner,
        )

    all_own(others).wait_recv()

    @pl.when(is_early)
    def _():
        for hh in range(HEADS):
            att_ref[:, hh * 128 : (hh + 1) * 128] = got_own[hh]

    @pl.when(is_late)
    def _():
        all_own_stat(others).wait_recv()
        all_far(everyone).wait_recv()
        all_far_stat(everyone).wait_recv()
        pad = jnp.zeros((128 - HEADS, 128), jnp.float32)
        stat_a = jnp.concatenate([got_stat_own[hh] for hh in range(HEADS)] + [pad], axis=0)
        stat_b = jnp.concatenate([got_stat_far[hh] for hh in range(HEADS)] + [pad], axis=0)
        lse_a = jnp.transpose(stat_a)[:GROUP]
        lse_b = jnp.transpose(stat_b)[:GROUP]
        share_a = 1.0 / (1.0 + jnp.exp2(lse_b - lse_a))
        share_b = 1.0 / (1.0 + jnp.exp2(lse_a - lse_b))
        for hh in range(HEADS):
            merged = (
                got_own[hh].astype(jnp.float32) * share_a[:, hh : hh + 1]
                + got_far[hh].astype(jnp.float32) * share_b[:, hh : hh + 1]
            )
            att_ref[:, hh * 128 : (hh + 1) * 128] = merged.astype(jnp.bfloat16)

    def col_arrived(j, carry):
        block = lax.rem(w + j, HALF)
        copy(
            column_out.at[block], column_in.at[block], col_send.at[block], col_recv.at[block],
            half_device(block),
        ).wait_recv()
        return carry

    lax.fori_loop(1, HALF, col_arrived, 0)
    heavy = column_in[0]
    for j in range(1, HALF):
        heavy = heavy + column_in[j]
    heavy_ref[...] = heavy

    for slot in range(7):
        k_copy(w, slot, w_core).wait_send()
        v_copy(w, slot, w_core).wait_send()

    all_own(others).wait_send()

    @pl.when(is_late)
    def _():
        all_own_stat(others).wait_send()

    @pl.when(is_early)
    def _():
        all_far(everyone).wait_send()
        all_far_stat(everyone).wait_send()

    def chunk_left(ci, carry):
        peer_copy(stat_own, ci).wait_send()

        @pl.when(is_late)
        def _():
            q_copy(ci).wait_send()

        return carry

    lax.fori_loop(0, CHUNKS, chunk_left, 0)

    def col_left(j, carry):
        col_copy(lax.rem(w + j, HALF)).wait_send()
        return carry

    lax.fori_loop(1, HALF, col_left, 0)


def hand_over_kernel(att_ref, heavy_ref, att_out, heavy_out):
    att_out[...] = att_ref[...]
    heavy_out[...] = heavy_ref[...]


def hand_over(attended, heavy):
    whole = pl.BlockSpec(memory_space=pltpu.VMEM)
    return pl.pallas_call(
        hand_over_kernel,
        out_shape=(
            jax.ShapeDtypeStruct(attended.shape, attended.dtype),
            jax.ShapeDtypeStruct(heavy.shape, heavy.dtype),
        ),
        in_specs=[whole] * 2,
        out_specs=(whole, whole),
    )(attended, heavy)


def local(queries, key_states, value_states):
    bf16, f32 = jnp.bfloat16, jnp.float32
    vmem, dma = pltpu.VMEM, pltpu.SemaphoreType.DMA
    whole = pl.BlockSpec(memory_space=pltpu.VMEM)
    attended, heavy = pl.pallas_call(
        kernel,
        out_shape=(
            jax.ShapeDtypeStruct((GROUP, HEADS * DIM), bf16),
            jax.ShapeDtypeStruct((1, ROWS), f32),
        ),
        in_specs=[pl.BlockSpec(memory_space=pl.ANY)] * 3,
        out_specs=(whole, whole),
        scratch_shapes=[
            vmem((HALF, ROWS, DIM), bf16),
            vmem((HALF, ROWS, DIM), bf16),
            vmem((ROWS, DIM), bf16),
            vmem((HALF, ROWS, ROWS), bf16),
            vmem((HALF, ROWS, 128), f32),
            vmem((HALF, ROWS, 128), f32),
            vmem((HALF, ROWS, DIM), f32),
            vmem((TILES, ROWS, WIDE), bf16),
            vmem((TILES, ROWS, 128), f32),
            vmem((TILES, CHUNK, 128), f32),
            vmem((TILES, CHUNK, DIM), f32),
            vmem((ROWS, 128), f32),
            vmem((HEADS, GROUP, DIM), bf16),
            vmem((HEADS, GROUP, DIM), bf16),
            vmem((CHUNKS, 1, 256), f32),
            vmem((CHUNKS, 1, 256), f32),
            vmem((CHUNKS, 1, 256), f32),
            vmem((HEADS, 1, 128), f32),
            vmem((HEADS, 1, 128), f32),
            vmem((HEADS, GROUP, DIM), bf16),
            vmem((HEADS, GROUP, DIM), bf16),
            vmem((HEADS, 1, 128), f32),
            vmem((HEADS, 1, 128), f32),
            vmem((HALF, 8, ROWS), f32),
            vmem((HALF, 1, ROWS), f32),
            vmem((HALF, 1, ROWS), f32),
            dma((7,)), dma((HALF,)), dma((7,)), dma((HALF,)), dma((CHUNKS,)), dma((CHUNKS,)),
            dma((1,)), dma((1,)), dma((1,)), dma((1,)),
            dma((1,)), dma((1,)), dma((1,)), dma((1,)),
            dma((CHUNKS,)), dma((CHUNKS,)), dma((HALF,)), dma((HALF,)),
            pltpu.SemaphoreType.REGULAR((4,)),
            dma((3,)),
            vmem((ROWS, DIM), bf16),
        ],
        compiler_params=pltpu.CompilerParams(
            collective_id=0, has_side_effects=True, vmem_limit_bytes=58 * 1024 * 1024
        ),
    )(queries, key_states, value_states)
    return hand_over(attended, heavy)


def solution(mesh):
    placed = (P("blk", "head"), P("blk", "head"), P("blk", "head"))
    return jax.shard_map(
        local,
        mesh=mesh,
        in_specs=placed,
        out_specs=(P(("blk", "head"), None), P("head", "blk")),
        check_vma=False,
    )
```

```python
import functools
import math

import jax
import jax.numpy as jnp
from jax import lax
from jax.experimental import pallas as pl
from jax.experimental.pallas import tpu as pltpu
from jax.sharding import PartitionSpec as P

MESH = pl.DeviceIdType.MESH
DIM = 128
ROWS = 768
HEADS = 32
HALF = 8
CHUNK = 192
CHUNKS = ROWS // CHUNK
GROUP = ROWS // HEADS
GROUPS = CHUNK // GROUP
TILE = 384
WIDE = 3072
PER = WIDE // ROWS
TILES = HALF // PER
SCALE = math.log2(math.e) / math.sqrt(DIM)
LOW = -1e30


def dot_rows(a, b):
    return lax.dot_general(a, b, (((1,), (1,)), ((), ())), preferred_element_type=jnp.float32)


def dot(a, b):
    return lax.dot_general(a, b, (((1,), (0,)), ((), ())), preferred_element_type=jnp.float32)


def fold_lanes(value, op):
    out = value[:, :128]
    for u in range(1, value.shape[1] // 128):
        out = op(out, value[:, u * 128 : (u + 1) * 128])
    return out


def weigh(logits, values):
    top = jnp.max(fold_lanes(logits, jnp.maximum), axis=1, keepdims=True)
    expo = jnp.exp2((logits - top) * SCALE)
    total = fold_lanes(expo, jnp.add)
    weights = expo.astype(jnp.bfloat16)
    return top, total, weights, dot(weights, values)


def to_lanes(column):
    out = []
    for begin, size in ((0, 128), (128, 64)):
        part = column[begin : begin + size]
        row = lax.broadcasted_iota(jnp.int32, part.shape, 0)
        lane = lax.broadcasted_iota(jnp.int32, part.shape, 1)
        out.append(jnp.sum(jnp.where(row == lane, part, 0.0), axis=0, keepdims=True))
    return out


def to_groups(column):
    parts = column.reshape(GROUPS, GROUP, 128)
    row = lax.broadcasted_iota(jnp.int32, parts.shape, 1)
    lane = lax.broadcasted_iota(jnp.int32, parts.shape, 2)
    return jnp.sum(jnp.where(row == lane, parts, 0.0), axis=1, keepdims=True)


def to_column(row):
    parts = []
    for begin, size in ((0, 128), (128, 64)):
        square = jnp.broadcast_to(row[:, begin : begin + 128], (128, 128))
        parts.append(jnp.transpose(square)[:size])
    return jnp.concatenate(parts, axis=0)


def kernel(
    q_ref, k_ref, v_ref, att_ref, heavy_ref,
    keys, values, q_far, weights_tri, top_tri, total_tri, out_tri,
    weights_far, top_far, total_far, out_far, lse_col,
    send_own, send_far, stat_own, stat_far, stat_peer,
    tag_own, tag_far, got_own, got_far, got_stat_own, got_stat_far,
    column, column_out, column_in,
    k_send, k_recv, v_send, v_recv, q_send, q_recv,
    own_send, own_recv, own_stat_send, own_stat_recv,
    far_send, far_recv, far_stat_send, far_stat_recv,
    peer_send, peer_recv, col_send, col_recv, ready, local_sem, q_own,
):
    h = lax.axis_index("head")
    b = lax.axis_index("blk")
    later = b // HALF
    w = lax.rem(b, HALF)
    y, core = w // 2, lax.rem(w, 2)
    x, z = h // 8, lax.rem(h, 8)
    base = later * HALF
    is_early, is_late = later == 0, later == 1

    def place(dy, flip):
        yy = lax.rem(y + dy, 4)
        return yy * 2 + (lax.rem(core + flip, 2))

    def half_device(block):
        return (h, base + block)

    partner = (h, w + (1 - later) * HALF)
    w_right, w_left, w_core = place(1, 0), place(3, 0), place(0, 1)

    def copy(src, dst, send_sem, recv_sem, device):
        return pltpu.make_async_remote_copy(
            src_ref=src, dst_ref=dst, send_sem=send_sem, recv_sem=recv_sem,
            device_id=device, device_id_type=MESH,
        )

    barrier = pltpu.get_barrier_semaphore()

    def greet(device):
        pl.semaphore_signal(barrier, inc=1, device_id=device, device_id_type=MESH)

    def along_z(step):
        return ((z >= step, (h - step, b)), (z + step < 8, (h + step, b)))

    def along_x():
        return [(lax.rem(h + 8 * d, HEADS), b) for d in (1, 2, 3)]

    def count_z(step):
        return (z >= step).astype(jnp.int32) + (z + step < 8).astype(jnp.int32)

    for exists, device in along_z(1):
        pl.when(exists)(functools.partial(greet, device))
    for device in along_x():
        greet(device)
    for block in (w_right, w_left, w_core):
        greet(half_device(block))
    pl.when(is_early)(functools.partial(greet, partner))

    def tell(index, device):
        pl.semaphore_signal(ready.at[index], inc=1, device_id=device, device_id_type=MESH)

    def tell_z(index, step):
        for exists, device in along_z(step):
            pl.when(exists)(functools.partial(tell, index, device))

    def hear(index, count):
        pl.semaphore_wait(ready.at[index], count)

    inside = [
        pltpu.make_async_copy(src, dst, local_sem.at[n])
        for n, (src, dst) in enumerate(((q_ref, q_own), (k_ref, keys.at[w]), (v_ref, values.at[w])))
    ]
    for one in inside:
        one.start()

    def triangle(block, masked, tiles):
        for t in tiles:
            rows = pl.ds(t * TILE, TILE)
            logits = dot_rows(q_own[rows, :], keys[block])
            if masked:
                row = lax.broadcasted_iota(jnp.int32, logits.shape, 0) + t * TILE
                col = lax.broadcasted_iota(jnp.int32, logits.shape, 1)
                logits = jnp.where(col <= row, logits, LOW)
            top, total, weights, out = weigh(logits, values[block])
            weights_tri[block, rows, :] = weights
            top_tri[block, rows, :] = jnp.broadcast_to(top, (TILE, 128))
            total_tri[block, rows, :] = total
            out_tri[block, rows, :] = out

    pl.semaphore_wait(barrier, 6 + count_z(1) + later)

    def q_copy(ci):
        rows = pl.ds(pl.multiple_of(ci * CHUNK, CHUNK), CHUNK)
        return copy(q_ref.at[rows], q_far.at[rows], q_send.at[ci], q_recv.at[ci], partner)

    def send_queries(i):
        pl.when(is_late)(lambda: q_copy(lax.rem(x + i, CHUNKS)).start())

    send_queries(0)

    def k_copy(block, slot, to):
        return copy(keys.at[block], keys.at[block], k_send.at[slot], k_recv.at[block], half_device(to))

    def v_copy(block, slot, to):
        return copy(values.at[block], values.at[block], v_send.at[slot], v_recv.at[block], half_device(to))

    def own_copy_out(src, dst, send_sem, recv_sem, slot, to):
        return copy(src, dst.at[w], send_sem.at[slot], recv_sem.at[w], half_device(to))

    def k_out(slot, to):
        own_copy_out(k_ref, keys, k_send, k_recv, slot, to).start()

    def v_out(slot, to):
        own_copy_out(v_ref, values, v_send, v_recv, slot, to).start()

    k_out(0, w_right)
    v_out(1, w_left)
    k_out(2, w_core)
    v_out(2, w_core)
    v_out(0, w_right)
    k_out(1, w_left)

    tell_z(0, 1)
    for one in inside:
        one.wait()
    triangle(w, True, (0,))
    hear(0, count_z(1))
    tell_z(1, 2)
    triangle(w, True, (1,))
    hear(1, count_z(2))
    tell_z(2, 4)
    send_queries(1)
    column[...] = jnp.zeros_like(column)

    def k_wait(block):
        k_copy(block, 0, w_core).wait_recv()

    def v_wait(block):
        v_copy(block, 0, w_core).wait_recv()

    k_wait(w_left)
    k_copy(w_left, 3, w_right).start()
    v_wait(w_right)
    v_copy(w_right, 3, w_left).start()

    def own_copy(hg):
        return copy(send_own.at[hg], got_own.at[h], own_send.at[hg], own_recv.at[h], (hg, b))

    def own_stat_copy(hg):
        return copy(
            tag_own.at[hg], got_stat_own.at[h],
            own_stat_send.at[hg], own_stat_recv.at[h], (hg, b),
        )

    def far_copy(hg):
        return copy(send_far.at[hg], got_far.at[h], far_send.at[hg], far_recv.at[h], (hg, w + HALF))

    def far_stat_copy(hg):
        return copy(
            tag_far.at[hg], got_stat_far.at[h],
            far_stat_send.at[hg], far_stat_recv.at[h], (hg, w + HALF),
        )

    def peer_copy(stat, ci):
        return copy(stat.at[ci], stat_peer.at[ci], peer_send.at[ci], peer_recv.at[ci], partner)

    def settle(count, rows, tops, totals, outs):
        top = lax.fori_loop(
            1, count, lambda j, top: jnp.maximum(top, tops[j, rows, :]), tops[0, rows, :]
        )

        def add(j, carry):
            total, out = carry
            factor = jnp.exp2((tops[j, rows, :] - top) * SCALE)
            return (total + factor * totals[j, rows, :], out + factor * outs[j, rows, :])

        zero = jnp.zeros((CHUNK, 128), jnp.float32)
        total, out = lax.fori_loop(0, count, add, (zero, zero))
        total = jnp.sum(total, axis=1, keepdims=True)
        return out * (1.0 / total), top * SCALE + jnp.log2(total)

    def settle_triangle():
        def chunk(ci, carry):
            rows = pl.ds(pl.multiple_of(ci * CHUNK, CHUNK), CHUNK)
            out, lse = settle(w + 1, rows, top_tri, total_tri, out_tri)
            send_own[pl.ds(ci * GROUPS, GROUPS)] = out.reshape(GROUPS, GROUP, DIM).astype(jnp.bfloat16)
            lse_col[rows, :] = lse
            tag_own[pl.ds(ci * GROUPS, GROUPS)] = to_groups(lse)
            low, high = to_lanes(lse)
            stat_own[ci, :, :128] = low
            stat_own[ci, :, 128:] = high
            return carry

        lax.fori_loop(0, CHUNKS, chunk, 0)

        @pl.when(is_late)
        def _():
            for ci in range(CHUNKS):
                peer_copy(stat_own, ci).start()

        got_own[h] = send_own[h]

        def start(j, carry):
            hg = lax.rem(h + j, HEADS)
            own_copy(hg).start()

            @pl.when(is_late)
            def _():
                own_stat_copy(hg).start()

            return carry

        lax.fori_loop(1, HEADS, start, 0)

        @pl.when(is_late)
        def _():
            got_stat_own[h] = tag_own[h]

    def rectangle(ci, first):
        q_copy(ci).wait_recv()
        rows = pl.ds(pl.multiple_of(ci * CHUNK, CHUNK), CHUNK)
        local = pl.ds(0, CHUNK)

        def step(d, carry):
            blocks = pl.ds(d * PER, PER)
            key_tile = keys[blocks].reshape(WIDE, DIM)
            value_tile = values[blocks].reshape(WIDE, DIM)
            logits = dot_rows(q_far[rows, :], key_tile)
            top, total, weights, out = weigh(logits, value_tile)
            weights_far[d, rows, :] = weights
            top_far[d, rows, :] = jnp.broadcast_to(top, (CHUNK, 128))
            total_far[d, local, :] = total
            out_far[d, local, :] = out
            return carry

        for d in range(TILES):
            step(d, 0)
        top = top_far[0, rows, :]
        for d in range(1, TILES):
            top = jnp.maximum(top, top_far[d, rows, :])
        total = jnp.zeros((CHUNK, 128), jnp.float32)
        out = jnp.zeros((CHUNK, 128), jnp.float32)
        for d in range(TILES):
            factor = jnp.exp2((top_far[d, rows, :] - top) * SCALE)
            total = total + factor * total_far[d]
            out = out + factor * out_far[d]
        total = jnp.sum(total, axis=1, keepdims=True)
        out = out * (1.0 / total)
        send_far[pl.ds(ci * GROUPS, GROUPS)] = out.reshape(GROUPS, GROUP, DIM).astype(jnp.bfloat16)
        lse = top * SCALE + jnp.log2(total)
        tag_far[pl.ds(ci * GROUPS, GROUPS)] = to_groups(lse)
        low, high = to_lanes(lse)
        stat_far[ci, :, :128] = low
        stat_far[ci, :, 128:] = high

        pl.when(first)(functools.partial(hear, 3, 1))

        def start(g, carry):
            hg = ci * GROUPS + lax.rem(z + g, GROUPS)
            far_copy(hg).start()
            far_stat_copy(hg).start()
            return carry

        lax.fori_loop(0, GROUPS, start, 0)
        peer_copy(stat_far, ci).start()

    def step(i, carry):
        @pl.when(i == 1)
        def _():
            hear(2, count_z(4))
            pl.when(is_late)(functools.partial(tell, 3, partner))
            k_wait(w_core)
            v_wait(w_core)

        @pl.when(i == 2)
        def _():
            k_copy(w_left, 4, w_core).start()
            v_copy(w_right, 5, w_core).start()
            send_queries(2)
            v_wait(w_left)
            v_copy(w_left, 4, w_core).start()
            k_wait(w_right)
            k_copy(w_right, 5, w_core).start()

        @pl.when(i == 4)
        def _():
            send_queries(3)
            for dy in (3, 1):
                k_wait(place(dy, 1))
                v_wait(place(dy, 1))

        @pl.when(i == 6)
        def _():
            far_block = place(2, 0)
            k_wait(far_block)
            k_copy(far_block, 6, w_core).start()
            v_wait(far_block)
            v_copy(far_block, 6, w_core).start()
            k_wait(place(2, 1))
            v_wait(place(2, 1))

        @pl.when(jnp.logical_and(is_early, jnp.logical_and(i >= 6, i != 9)))
        def _():
            rectangle(lax.rem(x + jnp.where(i < 9, i - 6, i - 7), CHUNKS), i == 6)

        def unit(u, carry):
            dy = jnp.where(u == 1, 0, jnp.where(u >= 6, 2, jnp.where(lax.rem(u, 2) == 0, 3, 1)))
            flip = jnp.where(jnp.logical_or(u == 1, jnp.logical_or(u == 4, jnp.logical_or(u == 5, u == 7))), 1, 0)
            block = place(dy, flip)

            @pl.when(block < w)
            def _():
                triangle(block, False, range(ROWS // TILE))

            return carry

        first = jnp.where(i <= 5, i, 6)
        last = jnp.where(i <= 5, i + 1, jnp.where(i == 9, 8, 6))
        lax.fori_loop(first, last, unit, 0)

        @pl.when(i == jnp.where(y <= 1, 5, 9))
        def _():
            settle_triangle()

        return carry

    lax.fori_loop(1, 11, step, 0)

    def add_columns(count, rows, tops, weights, lse, width):
        per = width // ROWS

        def tile(j, carry):
            factor = jnp.exp2(tops[j, rows, :] * SCALE - lse)
            for u in range(width // 128):
                part = weights[j, rows, u * 128 : (u + 1) * 128].astype(jnp.float32) * factor
                part = jnp.sum(part.reshape(CHUNK // 8, 8, 128), axis=0)
                lanes = slice(u % 6 * 128, u % 6 * 128 + 128)
                column[j * per + u // 6, :, lanes] += part
            return carry

        lax.fori_loop(0, count, tile, 0)

    def both(one, two):
        top = jnp.maximum(one, two)
        return top + jnp.log2(jnp.exp2(one - top) + jnp.exp2(two - top))

    def piece(i):
        ci = lax.rem(x + i, CHUNKS)
        return ci, pl.ds(pl.multiple_of(ci * CHUNK, CHUNK), CHUNK)

    @pl.when(is_early)
    def _():
        def near(i, carry):
            ci, rows = piece(i)
            add_columns(w + 1, rows, top_tri, weights_tri, lse_col[rows, :], ROWS)
            return carry

        lax.fori_loop(0, CHUNKS, near, 0)

        def distant(i, carry):
            ci, rows = piece(i)
            peer_copy(stat_own, ci).wait_recv()
            lse = to_column(both(stat_far[ci], stat_peer[ci]))
            add_columns(TILES, rows, top_far, weights_far, lse, WIDE)
            return carry

        lax.fori_loop(0, CHUNKS, distant, 0)

    @pl.when(is_late)
    def _():
        def near(i, carry):
            ci, rows = piece(i)
            peer_copy(stat_own, ci).wait_recv()
            lse = to_column(both(stat_own[ci], stat_peer[ci]))
            add_columns(w + 1, rows, top_tri, weights_tri, lse, ROWS)
            return carry

        lax.fori_loop(0, CHUNKS, near, 0)

    for j in range(HALF):
        column_out[j] = jnp.sum(column[j], axis=0, keepdims=True)

    def col_copy(block):
        return copy(
            column_out.at[block], column_in.at[w], col_send.at[block], col_recv.at[w], half_device(block)
        )

    def col_start(j, carry):
        col_copy(lax.rem(w + j, HALF)).start()
        return carry

    lax.fori_loop(1, HALF, col_start, 0)
    column_in[w] = column_out[w]

    def each(begin, wait):
        def one(j, carry):
            wait(lax.rem(h + j, HEADS))
            return carry

        lax.fori_loop(begin, HEADS, one, 0)

    def arrival(src, dst, send_sem, recv_sem, device):
        def wait(hg):
            copy(src.at[hg], dst.at[hg], send_sem.at[hg], recv_sem.at[hg], device).wait_recv()

        return wait

    near_by = half_device(w_core)
    each(1, arrival(send_own, got_own, own_send, own_recv, near_by))

    @pl.when(is_early)
    def _():
        for hh in range(HEADS):
            att_ref[:, hh * 128 : (hh + 1) * 128] = got_own[hh]

    @pl.when(is_late)
    def _():
        each(1, arrival(tag_own, got_stat_own, own_stat_send, own_stat_recv, near_by))
        each(0, arrival(send_far, got_far, far_send, far_recv, partner))
        each(0, arrival(tag_far, got_stat_far, far_stat_send, far_stat_recv, partner))
        pad = jnp.zeros((128 - HEADS, 128), jnp.float32)
        stat_a = jnp.concatenate([got_stat_own[hh] for hh in range(HEADS)] + [pad], axis=0)
        stat_b = jnp.concatenate([got_stat_far[hh] for hh in range(HEADS)] + [pad], axis=0)
        lse_a = jnp.transpose(stat_a)[:GROUP]
        lse_b = jnp.transpose(stat_b)[:GROUP]
        share_a = 1.0 / (1.0 + jnp.exp2(lse_b - lse_a))
        share_b = 1.0 / (1.0 + jnp.exp2(lse_a - lse_b))
        for hh in range(HEADS):
            merged = (
                got_own[hh].astype(jnp.float32) * share_a[:, hh : hh + 1]
                + got_far[hh].astype(jnp.float32) * share_b[:, hh : hh + 1]
            )
            att_ref[:, hh * 128 : (hh + 1) * 128] = merged.astype(jnp.bfloat16)

    def col_arrived(j, carry):
        block = lax.rem(w + j, HALF)
        copy(
            column_out.at[block], column_in.at[block], col_send.at[block], col_recv.at[block],
            half_device(block),
        ).wait_recv()
        return carry

    lax.fori_loop(1, HALF, col_arrived, 0)
    heavy = column_in[0]
    for j in range(1, HALF):
        heavy = heavy + column_in[j]
    heavy_ref[...] = heavy

    for slot in range(7):
        k_copy(w, slot, w_core).wait_send()
        v_copy(w, slot, w_core).wait_send()

    each(1, lambda hg: own_copy(hg).wait_send())

    @pl.when(is_late)
    def _():
        each(1, lambda hg: own_stat_copy(hg).wait_send())

    @pl.when(is_early)
    def _():
        each(0, lambda hg: far_copy(hg).wait_send())
        each(0, lambda hg: far_stat_copy(hg).wait_send())

    def chunk_left(ci, carry):
        peer_copy(stat_own, ci).wait_send()

        @pl.when(is_late)
        def _():
            q_copy(ci).wait_send()

        return carry

    lax.fori_loop(0, CHUNKS, chunk_left, 0)

    def col_left(j, carry):
        col_copy(lax.rem(w + j, HALF)).wait_send()
        return carry

    lax.fori_loop(1, HALF, col_left, 0)


def hand_over_kernel(att_ref, heavy_ref, att_out, heavy_out):
    att_out[...] = att_ref[...]
    heavy_out[...] = heavy_ref[...]


def hand_over(attended, heavy):
    whole = pl.BlockSpec(memory_space=pltpu.VMEM)
    return pl.pallas_call(
        hand_over_kernel,
        out_shape=(
            jax.ShapeDtypeStruct(attended.shape, attended.dtype),
            jax.ShapeDtypeStruct(heavy.shape, heavy.dtype),
        ),
        in_specs=[whole] * 2,
        out_specs=(whole, whole),
    )(attended, heavy)


def local(queries, key_states, value_states):
    bf16, f32 = jnp.bfloat16, jnp.float32
    vmem, dma = pltpu.VMEM, pltpu.SemaphoreType.DMA
    whole = pl.BlockSpec(memory_space=pltpu.VMEM)
    attended, heavy = pl.pallas_call(
        kernel,
        out_shape=(
            jax.ShapeDtypeStruct((GROUP, HEADS * DIM), bf16),
            jax.ShapeDtypeStruct((1, ROWS), f32),
        ),
        in_specs=[pl.BlockSpec(memory_space=pl.ANY)] * 3,
        out_specs=(whole, whole),
        scratch_shapes=[
            vmem((HALF, ROWS, DIM), bf16),
            vmem((HALF, ROWS, DIM), bf16),
            vmem((ROWS, DIM), bf16),
            vmem((HALF, ROWS, ROWS), bf16),
            vmem((HALF, ROWS, 128), f32),
            vmem((HALF, ROWS, 128), f32),
            vmem((HALF, ROWS, DIM), f32),
            vmem((TILES, ROWS, WIDE), bf16),
            vmem((TILES, ROWS, 128), f32),
            vmem((TILES, CHUNK, 128), f32),
            vmem((TILES, CHUNK, DIM), f32),
            vmem((ROWS, 128), f32),
            vmem((HEADS, GROUP, DIM), bf16),
            vmem((HEADS, GROUP, DIM), bf16),
            vmem((CHUNKS, 1, 256), f32),
            vmem((CHUNKS, 1, 256), f32),
            vmem((CHUNKS, 1, 256), f32),
            vmem((HEADS, 1, 128), f32),
            vmem((HEADS, 1, 128), f32),
            vmem((HEADS, GROUP, DIM), bf16),
            vmem((HEADS, GROUP, DIM), bf16),
            vmem((HEADS, 1, 128), f32),
            vmem((HEADS, 1, 128), f32),
            vmem((HALF, 8, ROWS), f32),
            vmem((HALF, 1, ROWS), f32),
            vmem((HALF, 1, ROWS), f32),
            dma((7,)), dma((HALF,)), dma((7,)), dma((HALF,)), dma((CHUNKS,)), dma((CHUNKS,)),
            dma((HEADS,)), dma((HEADS,)), dma((HEADS,)), dma((HEADS,)),
            dma((HEADS,)), dma((HEADS,)), dma((HEADS,)), dma((HEADS,)),
            dma((CHUNKS,)), dma((CHUNKS,)), dma((HALF,)), dma((HALF,)),
            pltpu.SemaphoreType.REGULAR((4,)),
            dma((3,)),
            vmem((ROWS, DIM), bf16),
        ],
        compiler_params=pltpu.CompilerParams(
            collective_id=0, has_side_effects=True, vmem_limit_bytes=58 * 1024 * 1024
        ),
    )(queries, key_states, value_states)
    return hand_over(attended, heavy)


def solution(mesh):
    placed = (P("blk", "head"), P("blk", "head"), P("blk", "head"))
    return jax.shard_map(
        local,
        mesh=mesh,
        in_specs=placed,
        out_specs=(P(("blk", "head"), None), P("head", "blk")),
        check_vma=False,
    )
```
